512 devices in a mesh: frow: 16 (over z), fcol: 32 (over x, y, core).
Axes of the slice: x: 4, y: 4, z: 16, core: 2. Of those that a mesh axis runs over, the one named last changes fastest.
Arguments:
- strips: bfloat16 [2, 16, 32, 64, 4096], P(None, 'frow', 'fcol'), may hold values from -0.09375 to 0.09375
- facet_window: float32 [16, 32, 256], P('frow', 'fcol'), may hold values from 0.25 to 4
- sub_offset: int32 [12], replicated, may hold values from 0 to 4095
- sub_owner: int32 [12], replicated, may hold values from 0 to 15, as said below
- block_tile: int32 [2048], P(('frow', 'fcol')), may hold values from 0 to 47
- vis_coords: float32 [2, 2048, 512], P(None, ('frow', 'fcol')), may hold values from -0.5 to 0.5
Outputs:
- subgrids: bfloat16 [16, 2, 2, 64, 256], P('frow')
- visibilities: float32 [2, 2048, 512], P(None, ('frow', 'fcol'))
The draws below stay inside these ranges and needn't reach their ends.
Inputs may be any that keep to these rules, and one draw needn't show every extreme that they name: `sub_owner`: no facet row index owns more than 2 listed subgrids, and one owns exactly 2; facet rows 0 and 15 each own at least one.
All inputs are finite; a program needn't handle non-finite values.
Results may differ from the reference program's by a relative error of at most 0.015.
Values may be sent and summed in bfloat16 or wider, within the bound.
A program may use at most 64 MiB of HBM per device.

```python
import math
import jax
import jax.numpy as jnp
from jax import lax

L = 4096
M = 256
TS = 64
VB = 512
CAP = 2
ROWS = 64
NB = 4
S = 12
TPS = 4
BLOCKS = 2048
N_FROW = 16
N_FCOL = 32


def draw_sub_owner(key, part):
    key = jax.random.fold_in(key, 7)
    first_key, spread_key, order_key = jax.random.split(key, 3)
    first = jax.random.randint(first_key, (), 0, 2, dtype=jnp.int32) * (N_FROW - 1)
    opposite = N_FROW - 1 - first
    packed_row = opposite - (opposite > first).astype(jnp.int32)
    forced_slot = packed_row * CAP
    pool = (N_FROW - 1) * CAP
    picks = jax.random.permutation(spread_key, pool - 1)[:S - CAP - 1].astype(jnp.int32)
    picks = picks + (picks >= forced_slot).astype(jnp.int32)
    slots = jnp.concatenate([jnp.full((1,), forced_slot, jnp.int32), picks])
    others = slots // CAP
    others = others + (others >= first).astype(jnp.int32)
    owners = jnp.concatenate([jnp.full((CAP,), first, jnp.int32), others.astype(jnp.int32)])
    order = jax.random.permutation(order_key, S)
    return owners[order].astype(jnp.int32)


def touch_ends(entries, rng, smallest, high):
    longest = entries.shape.index(max(entries.shape))
    spots = []
    for shift in (0, 1):
        where = [jax.random.randint(jax.random.fold_in(rng, axis), (), 0, length) for axis, length in enumerate(entries.shape)]
        where[longest] = (where[longest] + shift) % entries.shape[longest]
        spots.append(tuple(where))
    return entries.at[spots[0]].set(smallest).at[spots[1]].set(high)


def steps_of(rng, dims, shards, least, top_value):
    def one(dim, parts):
        steps = jax.random.uniform(jax.random.fold_in(jax.random.fold_in(rng, 6), dim), (parts,), jnp.float32, least / len(shards), top_value / len(shards))
        return jnp.repeat(jnp.exp(steps), dims[dim] // parts).reshape((-1,) + (1,) * (len(dims) - dim - 1))

    loudness = one(*shards[0])
    for cut in shards[1:]:
        loudness = loudness * one(*cut)
    return loudness


def normal_values(rng, dims, spread, limit, cuts=(), held_as=jnp.bfloat16):
    entries = jax.random.normal(rng, dims, jnp.float32) * spread
    if len(cuts) > 0:
        entries = steps_of(rng, dims, cuts, -0.22, 0.18) * entries
    return jnp.clip(entries, min=-limit, max=limit).astype(held_as)


def setup_inputs(seed: int = 0) -> dict:
    splits = jax.random.split(jax.random.key(seed), 7)
    strips = normal_values(splits[0], (2, N_FROW, N_FCOL, ROWS, L), L ** -0.5, 0.09375, ((1, 16), (2, 32)))
    facet_window = jnp.clip(jnp.exp(math.log(4.0) - 2.7725887 * jax.random.uniform(splits[1], (N_FROW, N_FCOL, M), jnp.float32) ** steps_of(splits[1], (N_FROW, N_FCOL, M), ((0, 16), (1, 32)), -0.2, 0.2)), 0.25, 4.0)
    sub_offset = touch_ends(jax.random.randint(splits[2], (S,), 0, L), jax.random.fold_in(splits[2], 1), 0, L - 1).astype(jnp.int32)
    sub_owner = draw_sub_owner(jax.random.fold_in(splits[6], 71), 0)
    block_tile = touch_ends(jax.random.randint(splits[4], (BLOCKS,), 0, S * TPS), jax.random.fold_in(splits[4], 1), 0, (S * TPS) - 1).astype(jnp.int32)
    vis_coords = jnp.clip(jax.random.uniform(splits[5], (2, BLOCKS, VB), jnp.float32, -0.5, 0.5) * steps_of(splits[5], (2, BLOCKS, VB), ((1, 512),), -0.4, 0.0), -0.5, 0.5)
    return {"strips": strips, "facet_window": facet_window, "sub_offset": sub_offset, "sub_owner": sub_owner, "block_tile": block_tile, "vis_coords": vis_coords}


TWO_PI = 2.0 * math.pi

def facet_tables(shift_amount, total_len, contrib_cols):
    columns = jnp.arange(contrib_cols, dtype=jnp.int32)
    sample_points = jnp.arange(total_len, dtype=jnp.int32)
    freq_index = (shift_amount + columns) % total_len
    phase_index = sample_points[:, None] * freq_index[None, :] % total_len
    angles = phase_index.astype(jnp.float32) * (TWO_PI / total_len)
    return jnp.concatenate([jnp.cos(angles), jnp.sin(angles)], axis=1).astype(jnp.bfloat16)

def facet_contrib(strip_rows, window_row, table_one, row_count, col_count):
    product = jnp.dot(strip_rows, table_one, preferred_element_type=jnp.float32)
    real_part = product[:row_count, :col_count] - product[row_count:, col_count:]
    imag_part = product[:row_count, col_count:] + product[row_count:, :col_count]
    return (jnp.stack([real_part, imag_part]) * window_row).astype(jnp.bfloat16)

def owner_slots(sub_owner):
    count = sub_owner.shape[0]
    index = jnp.arange(count, dtype=jnp.int32)
    same = (sub_owner[:, None] == sub_owner[None, :]) & (index[None, :] < index[:, None])
    return lax.optimization_barrier(jnp.sum(same.astype(jnp.int32), axis=1)).astype(jnp.int32)

def degrid(tiles, coords, tile_side):
    frequency = jnp.arange(tile_side, dtype=jnp.float32) * TWO_PI
    along_row = frequency[None, :, None] * coords[0][:, None, :]
    along_col = frequency[None, :, None] * coords[1][:, None, :]
    cosine_column = jnp.cos(along_col).astype(jnp.bfloat16).astype(jnp.float32)
    sine_column = (-jnp.sin(along_col)).astype(jnp.bfloat16).astype(jnp.float32)
    cos_row = jnp.cos(along_row)
    sin_row = -jnp.sin(along_row)
    real_tile = tiles[:, 0].astype(jnp.float32)
    imag_tile = tiles[:, 1].astype(jnp.float32)

    def batched(left_factor, right_factor):
        return jnp.einsum('xul,xlj->xuj', left_factor, right_factor)
    half_real = batched(real_tile, cosine_column) - batched(imag_tile, sine_column)
    half_imag = batched(real_tile, sine_column) + batched(imag_tile, cosine_column)
    vis_real = lax.optimization_barrier(jnp.sum(cos_row * half_real - sin_row * half_imag, axis=1)) / tile_side
    vis_imag = lax.optimization_barrier(jnp.sum(cos_row * half_imag + sin_row * half_real, axis=1)) / tile_side
    return jnp.stack([vis_real, vis_imag])

def cut_tiles(stacked_grids, grid_index, tile_row, tile_col, side):

    def single(index, row_pos, col_pos):
        zero_start = index * 0
        starts = (index, zero_start, row_pos * side, col_pos * side)
        return lax.dynamic_slice(stacked_grids, starts, (1, 2, side, side))[0]
    return jax.vmap(single)(grid_index, tile_row, tile_col)

def reference(strips, facet_window, sub_offset, sub_owner, block_tile, vis_coords):
    facets = N_FROW * N_FCOL
    flat_strips = strips.reshape(2, facets, ROWS, L)
    flat_window = facet_window.reshape(facets, M)
    tables = [facet_tables(sub_offset[index], L, M) for index in range(S)]

    def add_facet(facet, total):
        strip = lax.dynamic_index_in_dim(flat_strips, facet, 1, keepdims=False)
        window_row = lax.dynamic_index_in_dim(flat_window, facet, 0, keepdims=False)
        strip_rows = strip.reshape(2 * ROWS, L)
        pieces = [lax.optimization_barrier(facet_contrib(strip_rows, window_row, table, ROWS, M)).astype(jnp.float32) for table in tables]
        return total + jnp.stack(pieces)
    total = lax.fori_loop(0, facets, add_facet, jnp.zeros((S, 2, ROWS, M), jnp.float32))
    grids = (total * (1.0 / math.sqrt(facets))).astype(jnp.bfloat16)
    slot_of = owner_slots(sub_owner)
    target = (sub_owner * CAP + slot_of).astype(jnp.int32)
    placed = jnp.zeros((N_FROW * CAP, 2, ROWS, M), jnp.bfloat16).at[target].set(grids)
    subgrids = placed.reshape(N_FROW, CAP, 2, ROWS, M)
    tiles_across = M // TS
    groups = BLOCKS // NB
    tile_ids = block_tile.reshape(groups, NB)
    coord_groups = vis_coords.reshape(2, groups, NB, VB)

    def one_group(group):
        ids = lax.dynamic_index_in_dim(tile_ids, group, 0, keepdims=False)
        coords = lax.dynamic_index_in_dim(coord_groups, group, 1, keepdims=False)
        sub_index = (ids // TPS).astype(jnp.int32)
        within = ids % TPS
        tile_row = (within // tiles_across).astype(jnp.int32)
        tile_col = (within % tiles_across).astype(jnp.int32)
        tiles = cut_tiles(grids, sub_index, tile_row, tile_col, TS)
        return degrid(tiles, coords, TS)
    result = lax.map(one_group, jnp.arange(groups, dtype=jnp.int32))
    visibilities = jnp.transpose(result, (1, 0, 2, 3)).reshape(2, BLOCKS, VB)
    return (subgrids, visibilities)
```

```python
import math

import jax
import jax.numpy as jnp
import numpy as np
from jax import lax
from jax.experimental import pallas as pl
from jax.experimental.pallas import tpu as pltpu
from jax.sharding import PartitionSpec as P

MESH = pl.DeviceIdType.MESH
TS = 64
CAP = 2
ROWS = 64
M = 256
L = 4096
S = 12
RADIX = 16
NB = 4
VB = 512
CHUNKS = 3
GROUP = 32
FAR = 8


def dft_table():
    index = np.arange(M)
    angle = 2.0 * np.pi * ((index[:, None] * index[None, :]) % M) / M
    return np.concatenate([np.cos(angle), np.sin(angle)], axis=1).astype(jnp.bfloat16)


def twiddle_table():
    angle = 2.0 * np.pi * np.arange(RADIX)[:, None] * np.arange(M)[None, :] / L
    return np.stack([np.cos(angle), np.sin(angle)]).astype(np.float32)


def half_turn_polynomials():
    nodes = 0.5 * np.cos(np.pi * (np.arange(400) + 0.5) / 800)
    square = nodes * nodes
    sine = np.polynomial.polynomial.polyfit(square, np.sin(np.pi * nodes) / nodes, 5)
    cosine = np.polynomial.polynomial.polyfit(square, np.cos(np.pi * nodes), 5)
    return [float(v) for v in sine], [float(v) for v in cosine]


SINE, COSINE = half_turn_polynomials()


def turn_cos_sin(turns):
    r = turns - jnp.floor(turns + 0.5)
    u = r * r
    s = jnp.full_like(u, SINE[-1])
    c = jnp.full_like(u, COSINE[-1])
    for a, b in zip(SINE[-2::-1], COSINE[-2::-1]):
        s = s * u + a
        c = c * u + b
    s = s * r
    twice = s + s
    return 1.0 - twice * s, twice * c


def times_root(re, im, power):
    power = power % 16
    if power == 0:
        return re, im
    if power == 4:
        return -im, re
    if power == 8:
        return -re, -im
    if power == 12:
        return im, -re
    c = math.cos(2.0 * math.pi * power / 16)
    s = math.sin(2.0 * math.pi * power / 16)
    if power in (2, 6, 10, 14):
        a = abs(c)
        plus, minus = (re + im) * a, (re - im) * a
        return {2: (minus, plus), 6: (-plus, minus), 10: (-minus, -plus), 14: (plus, -minus)}[power]
    return re * c - im * s, re * s + im * c


def dft4(v):
    (ar, ai), (br, bi), (cr, ci), (dr, di) = v
    pr, pi_, qr, qi = ar + cr, ai + ci, ar - cr, ai - ci
    sr, si, tr, ti = br + dr, bi + di, br - dr, bi - di
    return [(pr + sr, pi_ + si), (qr - ti, qi + tr), (pr - sr, pi_ - si), (qr + ti, qi - tr)]


def dft16(x):
    inner = []
    for low in range(4):
        inner.append(dft4([x[4 * high + low] for high in range(4)]))
    out = [None] * 16
    for c0 in range(4):
        column = [times_root(*inner[low][c0], low * c0) for low in range(4)]
        for c1, value in enumerate(dft4(column)):
            out[4 * c1 + c0] = value
    return out


def kernel(
    off_ref, own_ref, tile_ref, strips_hbm, window_ref, coords_ref, table_ref, twiddle_ref,
    sub_ref, vis_ref,
    strips, zb, xt, con, theirs, merged, near, far, grid, row_phase, col_cos, col_sin,
    load_sem, core_s, core_r, near_s, near_r, far_s, far_r, all_s, all_r, fwd_s, fwd_r,
):
    z = lax.axis_index("frow")
    f = lax.axis_index("fcol")
    core = lax.rem(f, 2)
    chip = f // 2
    x, y = chip // 4, lax.rem(chip, 4)
    side = lax.rem(z, 2)
    ring = z // 2
    sibling = f + 1 - 2 * core

    def loads(part):
        rows = pl.ds(16 * part, 16)
        return pltpu.make_async_copy(strips_hbm.at[:, rows], strips.at[:, rows], load_sem.at[part])

    for part in range(4):
        loads(part).start()

    def partner(k):
        dz, kk = k // 16, lax.rem(k, 16)
        to_x = lax.rem(x + kk // 4, 4)
        to_y = lax.rem(y + lax.rem(kk, 4), 4)
        to_chip = 4 * to_x + to_y
        to_side = lax.rem(side + dz, 2)
        return to_chip, to_side, {"frow": 2 * ring + to_side, "fcol": 2 * to_chip + core}

    def along(k):
        return {"frow": 2 * lax.rem(ring + k, FAR) + side, "fcol": f}

    sib = {"frow": z, "fcol": sibling}
    barrier = pltpu.get_barrier_semaphore()
    pl.semaphore_signal(barrier, inc=1, device_id=sib, device_id_type=MESH)

    @pl.loop(1, GROUP)
    def _(k):
        pl.semaphore_signal(barrier, inc=1, device_id=partner(k)[2], device_id_type=MESH)

    @pl.loop(1, FAR)
    def _(k):
        pl.semaphore_signal(barrier, inc=1, device_id=along(k), device_id_type=MESH)

    def remote(src, dst, send, recv, where):
        return pltpu.make_async_remote_copy(
            src_ref=src, dst_ref=dst, send_sem=send, recv_sem=recv, device_id=where, device_id_type=MESH
        )

    for part in range(4):
        loads(part).wait()
        rows = pl.ds(16 * part, 16)
        low_rows = pl.ds(ROWS + 16 * part, 16)

        @pl.loop(0, 2)
        def _(half):
            lane = pl.multiple_of(half * 128, 128)
            samples = []
            for g in range(RADIX):
                lanes = pl.ds(pl.multiple_of(M * g + lane, 128), 128)
                samples.append((strips[0, rows, lanes].astype(jnp.float32), strips[1, rows, lanes].astype(jnp.float32)))
            first = pl.ds(lane, 128)
            second = pl.ds(pl.multiple_of(M + lane, 128), 128)
            for c, (re, im) in enumerate(dft16(samples)):
                if c:
                    cos = twiddle_ref[0, pl.ds(c, 1), first]
                    sin = twiddle_ref[1, pl.ds(c, 1), first]
                    re, im = re * cos - im * sin, re * sin + im * cos
                re16, im16 = re.astype(jnp.bfloat16), im.astype(jnp.bfloat16)
                zb[c, rows, first] = re16
                zb[c, rows, second] = -im16
                zb[c, low_rows, first] = im16
                zb[c, low_rows, second] = re16

    for pair in range(RADIX // 2):
        both = zb[2 * pair : 2 * pair + 2].reshape(2 * 128, 2 * M)
        product = lax.dot_general(
            table_ref[...], both, (((1,), (1,)), ((), ())), preferred_element_type=jnp.float32
        )
        for e in range(2):
            c = 2 * pair + e
            piece = product[:, 128 * e : 128 * e + 128]
            xt[pl.ds(c, M, stride=RADIX), :] = piece
            xt[pl.ds(L + c, M // RADIX, stride=RADIX), :] = piece[: M // RADIX]

    window = jnp.transpose(jnp.broadcast_to(window_ref[...], (128, M)))

    for j in range(CHUNKS):
        for q in range(4):
            s = 4 * j + q
            con[s] = (xt[pl.ds(off_ref[s], M), :] * window).astype(jnp.bfloat16)
        if j == 0:
            pl.semaphore_wait(barrier, 1 + (GROUP - 1) + (FAR - 1))
        for e in range(2):
            h = 2 * j + e
            remote(con.at[2 * h + 1 - core], theirs.at[h], core_s.at[h], core_r.at[h], sib).start()

    def near_copy(j, k):
        to_chip, to_side, where = partner(k)
        src = merged.at[2 * j + to_side, pl.ds(pl.multiple_of(16 * to_chip, 16), 16)]
        return remote(src, near.at[j, k], near_s.at[j], near_r.at[j], where)

    for j in range(CHUNKS):
        for e in range(2):
            h = 2 * j + e
            remote(con.at[2 * h + 1 - core], theirs.at[h], core_s.at[h], core_r.at[h], sib).wait_recv()
            merged[h] = (con[2 * h + core].astype(jnp.float32) + theirs[h].astype(jnp.float32)).astype(jnp.bfloat16)

        @pl.loop(1, GROUP)
        def _(k):
            near_copy(j, k).start()

    steps = lax.broadcasted_iota(jnp.int32, (TS, 128), 0).astype(jnp.float32)

    @pl.loop(0, VB // 128)
    def _(block):
        lanes = pl.ds(pl.multiple_of(128 * block, 128), 128)
        later = pl.ds(pl.multiple_of(VB + 128 * block, 128), 128)
        for k in range(NB):
            cos, sin = turn_cos_sin(steps * coords_ref[0, k : k + 1, lanes])
            cos, sin = cos.astype(jnp.bfloat16), sin.astype(jnp.bfloat16)
            row_phase[k, 0:TS, lanes] = cos
            row_phase[k, TS : 2 * TS, lanes] = sin
            row_phase[k, 0:TS, later] = -sin
            row_phase[k, TS : 2 * TS, later] = cos
            cos, sin = turn_cos_sin(steps * coords_ref[1, k : k + 1, lanes])
            col_cos[k, :, lanes] = cos
            col_sin[k, :, lanes] = sin

    mine = pl.ds(pl.multiple_of(16 * chip, 16), 16)

    def far_copy(j, k):
        return remote(far.at[j, ring], far.at[j, ring], far_s.at[j], far_r.at[j], along(k))

    def all_copy(j, k):
        at = grid.at[4 * (2 * (2 * j + side) + core) + chip // 4, pl.ds(pl.multiple_of(16 * lax.rem(chip, 4), 16), 16)]
        return remote(at, at, all_s.at[j], all_r.at[j], partner(k)[2])

    def fwd_copy(j, e, half):
        at = grid.at[pl.ds(4 * (2 * (2 * j + e) + half), 4)]
        return remote(at, at, fwd_s.at[j, e], fwd_r.at[j, e], sib)

    def wait_for(buffer, sem):
        pltpu.make_async_copy(buffer, buffer, sem).wait()

    for j in range(CHUNKS):
        wait_for(near.at[j, pl.ds(1, GROUP - 1)], near_r.at[j])
        total = merged[2 * j + side, mine].astype(jnp.float32)
        for k in range(1, GROUP):
            total = total + near[j, k].astype(jnp.float32)
        far[j, ring] = total.astype(jnp.bfloat16)

        @pl.loop(1, FAR)
        def _(k):
            far_copy(j, k).start()

    scale = 1.0 / math.sqrt(512)
    for j in range(CHUNKS):
        wait_for(far.at[j, pl.ds(1, FAR - 1)], far_r.at[j])
        total = far[j, 0].astype(jnp.float32)
        for k in range(1, FAR):
            total = total + far[j, k].astype(jnp.float32)
        grid[4 * (2 * (2 * j + side) + core) + chip // 4, pl.ds(pl.multiple_of(16 * lax.rem(chip, 4), 16), 16)] = (
            total * scale
        ).astype(jnp.bfloat16)

        @pl.loop(1, GROUP)
        def _(k):
            all_copy(j, k).start()

    for j in range(CHUNKS):
        wait_for(near.at[j, pl.ds(1, GROUP - 1)], all_r.at[j])
        for e in range(2):
            fwd_copy(j, e, core).start()

    for j in range(CHUNKS):
        for e in range(2):
            fwd_copy(j, e, 1 - core).wait_recv()

    count = jnp.int32(0)
    place = [jnp.int32(0)] * CAP
    for s in range(S):
        hit = (own_ref[s] == z).astype(jnp.int32)
        for slot in range(CAP):
            place[slot] = place[slot] + jnp.where((hit == 1) & (count == slot), s, 0)
        count = count + hit
    for slot in range(CAP):
        picked = grid[pl.ds(4 * place[slot], 4)].reshape(M, 2 * ROWS).astype(jnp.float32)
        picked = jnp.where(count > slot, picked, 0.0)
        sub_ref[slot] = jnp.transpose(picked).astype(jnp.bfloat16)

    for k in range(NB):
        tile = grid[tile_ref[k]]
        half = jnp.dot(tile, row_phase[k], preferred_element_type=jnp.float32)
        re, im = half[:, :VB], half[:, VB:]
        cos, sin = col_cos[k], col_sin[k]
        vis_ref[0, pl.ds(k, 1)] = jnp.sum(re * cos + im * sin, axis=0, keepdims=True) * (1.0 / TS)
        vis_ref[1, pl.ds(k, 1)] = jnp.sum(im * cos - re * sin, axis=0, keepdims=True) * (1.0 / TS)

    for j in range(CHUNKS):
        for e in range(2):
            h = 2 * j + e
            remote(con.at[2 * h + 1 - core], theirs.at[h], core_s.at[h], core_r.at[h], sib).wait_send()
            fwd_copy(j, e, core).wait_send()
        wait_for(near.at[j, pl.ds(1, GROUP - 1)], near_s.at[j])
        wait_for(far.at[j, pl.ds(1, FAR - 1)], far_s.at[j])
        wait_for(near.at[j, pl.ds(1, GROUP - 1)], all_s.at[j])


def on_device(strips, facet_window, sub_offset, sub_owner, block_tile, vis_coords):
    smem = pl.BlockSpec(memory_space=pltpu.SMEM)
    vmem = pl.BlockSpec(memory_space=pltpu.VMEM)
    dma = pltpu.SemaphoreType.DMA
    bf16, f32 = jnp.bfloat16, jnp.float32
    subgrids, visibilities = pl.pallas_call(
        kernel,
        out_shape=(
            jax.ShapeDtypeStruct((CAP, 2 * ROWS, M), bf16),
            jax.ShapeDtypeStruct((2, NB, VB), f32),
        ),
        in_specs=[smem, smem, smem, pl.BlockSpec(memory_space=pl.ANY), vmem, vmem, vmem, vmem],
        out_specs=(vmem, vmem),
        scratch_shapes=[
            pltpu.VMEM((2, ROWS, L), bf16),
            pltpu.VMEM((RADIX, 2 * ROWS, 2 * M), bf16),
            pltpu.VMEM((L + M, 2 * ROWS), f32),
            pltpu.VMEM((S, M, 2 * ROWS), bf16),
            pltpu.VMEM((S // 2, M, 2 * ROWS), bf16),
            pltpu.VMEM((S // 2, M, 2 * ROWS), bf16),
            pltpu.VMEM((CHUNKS, GROUP, 16, 2 * ROWS), bf16),
            pltpu.VMEM((CHUNKS, FAR, 16, 2 * ROWS), bf16),
            pltpu.VMEM((4 * S, TS, 2 * ROWS), bf16),
            pltpu.VMEM((NB, 2 * TS, 2 * VB), bf16),
            pltpu.VMEM((NB, TS, VB), f32),
            pltpu.VMEM((NB, TS, VB), f32),
            dma((4,)),
            dma((S // 2,)), dma((S // 2,)),
            dma((CHUNKS,)), dma((CHUNKS,)),
            dma((CHUNKS,)), dma((CHUNKS,)),
            dma((CHUNKS,)), dma((CHUNKS,)),
            dma((CHUNKS, 2)), dma((CHUNKS, 2)),
        ],
        compiler_params=pltpu.CompilerParams(
            collective_id=0, has_side_effects=True, vmem_limit_bytes=40 * 2**20
        ),
        name="predict",
    )(
        sub_offset, sub_owner, block_tile, strips.reshape(2, ROWS, L), facet_window.reshape(1, M), vis_coords,
        jnp.asarray(dft_table()), jnp.asarray(twiddle_table()),
    )
    return subgrids.reshape(1, CAP, 2, ROWS, M), visibilities


def solution(mesh):
    placed = (
        P(None, "frow", "fcol", None, None),
        P("frow", "fcol", None),
        P(),
        P(),
        P(("frow", "fcol")),
        P(None, ("frow", "fcol"), None),
    )
    return jax.shard_map(
        on_device,
        mesh=mesh,
        in_specs=placed,
        out_specs=(P("frow", None, None, None, None), P(None, ("frow", "fcol"), None)),
        check_vma=False,
    )
```

```python
import math

import jax
import jax.numpy as jnp
import numpy as np
from jax import lax
from jax.experimental import pallas as pl
from jax.experimental.pallas import tpu as pltpu
from jax.sharding import PartitionSpec as P

MESH = pl.DeviceIdType.MESH
TS = 64
CAP = 2
ROWS = 64
M = 256
L = 4096
S = 12
RADIX = 16
NB = 4
VB = 512
CHUNKS = 3
GROUP = 32
FAR = 8
DIRECT = (2,)


def dft_table():
    index = np.arange(M)
    angle = 2.0 * np.pi * ((index[:, None] * index[None, :]) % M) / M
    return np.concatenate([np.cos(angle), np.sin(angle)], axis=1).astype(jnp.bfloat16)


def twiddle_table():
    angle = 2.0 * np.pi * np.arange(RADIX)[:, None] * np.arange(M)[None, :] / L
    return np.stack([np.cos(angle), np.sin(angle)]).astype(np.float32)


def half_turn_polynomials():
    nodes = 0.5 * np.cos(np.pi * (np.arange(400) + 0.5) / 800)
    square = nodes * nodes
    sine = np.polynomial.polynomial.polyfit(square, np.sin(np.pi * nodes) / nodes, 5)
    cosine = np.polynomial.polynomial.polyfit(square, np.cos(np.pi * nodes), 5)
    return [float(v) for v in sine], [float(v) for v in cosine]


SINE, COSINE = half_turn_polynomials()


def turn_cos_sin(turns):
    r = turns - jnp.floor(turns + 0.5)
    u = r * r
    s = jnp.full_like(u, SINE[-1])
    c = jnp.full_like(u, COSINE[-1])
    for a, b in zip(SINE[-2::-1], COSINE[-2::-1]):
        s = s * u + a
        c = c * u + b
    s = s * r
    twice = s + s
    return 1.0 - twice * s, twice * c


def times_root(re, im, power):
    power = power % 16
    if power == 0:
        return re, im
    if power == 4:
        return -im, re
    if power == 8:
        return -re, -im
    if power == 12:
        return im, -re
    c = math.cos(2.0 * math.pi * power / 16)
    s = math.sin(2.0 * math.pi * power / 16)
    if power in (2, 6, 10, 14):
        a = abs(c)
        plus, minus = (re + im) * a, (re - im) * a
        return {2: (minus, plus), 6: (-plus, minus), 10: (-minus, -plus), 14: (plus, -minus)}[power]
    return re * c - im * s, re * s + im * c


def dft4(v):
    (ar, ai), (br, bi), (cr, ci), (dr, di) = v
    pr, pi_, qr, qi = ar + cr, ai + ci, ar - cr, ai - ci
    sr, si, tr, ti = br + dr, bi + di, br - dr, bi - di
    return [(pr + sr, pi_ + si), (qr - ti, qi + tr), (pr - sr, pi_ - si), (qr + ti, qi - tr)]


def dft16(x):
    inner = []
    for low in range(4):
        inner.append(dft4([x[4 * high + low] for high in range(4)]))
    out = [None] * 16
    for c0 in range(4):
        column = [times_root(*inner[low][c0], low * c0) for low in range(4)]
        for c1, value in enumerate(dft4(column)):
            out[4 * c1 + c0] = value
    return out


def far_first(i):
    return (i + 2) * (1 - i // 2) + (3 - i) * (i // 2)


def kernel(
    off_hbm, own_hbm, tile_hbm, strips_hbm, window_hbm, coords_hbm, table_hbm, twiddle_hbm,
    sub_ref, vis_ref,
    off_ref, own_ref, tile_ref, strips, window_ref, coords_ref, table_ref, twiddle_ref, zb, xt, con, theirs, merged, near, far, grid, row_phase, col_cos, col_sin,
    load_sem, core_s, core_r, near_s, near_r, far_s, far_r, all_s, all_r, fwd_s, fwd_r, oth_s, oth_r,
):
    z = lax.axis_index("frow")
    f = lax.axis_index("fcol")
    core = lax.rem(f, 2)
    chip = f // 2
    x, y = chip // 4, lax.rem(chip, 4)
    side = lax.rem(z, 2)
    ring = z // 2
    sibling = f + 1 - 2 * core

    def loads(part):
        rows = pl.ds(16 * part, 16)
        return pltpu.make_async_copy(strips_hbm.at[:, rows], strips.at[:, rows], load_sem.at[part])

    def whole(src, dst, n):
        return pltpu.make_async_copy(src, dst, load_sem.at[4 + n])

    twiddles = whole(twiddle_hbm, twiddle_ref, 0)
    table = whole(table_hbm, table_ref, 1)
    windows = whole(window_hbm, window_ref, 2)
    coords = whole(coords_hbm, coords_ref, 3)
    offsets = whole(off_hbm, off_ref, 4)
    owners = whole(own_hbm, own_ref, 5)
    tiles = whole(tile_hbm, tile_ref, 6)
    loads(0).start()
    twiddles.start()
    for part in range(1, 4):
        loads(part).start()
    table.start()

    def place_of(k):
        to_x = lax.rem(x + far_first(k // 8), 4)
        to_y = lax.rem(y + far_first(lax.rem(k // 2, 4)), 4)
        to_chip = 4 * to_x + to_y
        to_side = lax.rem(side + 1 - lax.rem(k, 2), 2)
        return to_chip, to_side

    def partner(k, other):
        to_chip, to_side = place_of(k)
        to_core = 1 - core if other else core
        return {"frow": 2 * ring + to_side, "fcol": 2 * to_chip + to_core}

    def along(k):
        step = 4 + (k + 1) // 2 * (2 * lax.rem(k + 1, 2) - 1)
        return {"frow": 2 * lax.rem(ring + step, FAR) + side, "fcol": f}

    sib = {"frow": z, "fcol": sibling}
    barrier = pltpu.get_barrier_semaphore()

    @pl.loop(0, FAR - 1)
    def _(k):
        pl.semaphore_signal(barrier, inc=1, device_id=along(k), device_id_type=MESH)

    @pl.loop(0, GROUP - 1)
    def _(k):
        pl.semaphore_signal(barrier, inc=1, device_id=partner(k, 0), device_id_type=MESH)
        pl.semaphore_signal(barrier, inc=1, device_id=partner(k, 1), device_id_type=MESH)

    pl.semaphore_signal(barrier, inc=1, device_id=sib, device_id_type=MESH)
    for load in (offsets, windows, coords, owners, tiles):
        load.start()

    def remote(src, dst, send, recv, where):
        return pltpu.make_async_remote_copy(
            src_ref=src, dst_ref=dst, send_sem=send, recv_sem=recv, device_id=where, device_id_type=MESH
        )

    twiddles.wait()
    for part in range(4):
        loads(part).wait()
        rows = pl.ds(16 * part, 16)
        low_rows = pl.ds(ROWS + 16 * part, 16)

        @pl.loop(0, 2)
        def _(half):
            lane = pl.multiple_of(half * 128, 128)
            samples = []
            for g in range(RADIX):
                lanes = pl.ds(pl.multiple_of(M * g + lane, 128), 128)
                samples.append((strips[0, rows, lanes].astype(jnp.float32), strips[1, rows, lanes].astype(jnp.float32)))
            first = pl.ds(lane, 128)
            second = pl.ds(pl.multiple_of(M + lane, 128), 128)
            for c, (re, im) in enumerate(dft16(samples)):
                if c:
                    cos = twiddle_ref[0, pl.ds(c, 1), first]
                    sin = twiddle_ref[1, pl.ds(c, 1), first]
                    re, im = re * cos - im * sin, re * sin + im * cos
                re16, im16 = re.astype(jnp.bfloat16), im.astype(jnp.bfloat16)
                zb[c, rows, first] = re16
                zb[c, rows, second] = -im16
                zb[c, low_rows, first] = im16
                zb[c, low_rows, second] = re16

    table.wait()
    for pair in range(RADIX // 2):
        both = zb[2 * pair : 2 * pair + 2].reshape(2 * 128, 2 * M)
        product = lax.dot_general(
            table_ref[...], both, (((1,), (1,)), ((), ())), preferred_element_type=jnp.float32
        )
        for e in range(2):
            c = 2 * pair + e
            piece = product[:, 128 * e : 128 * e + 128]
            xt[pl.ds(c, M, stride=RADIX), :] = piece
            xt[pl.ds(L + c, M // RADIX, stride=RADIX), :] = piece[: M // RADIX]

    windows.wait()
    offsets.wait()
    window = jnp.transpose(jnp.broadcast_to(window_ref[...], (128, M)))

    for j in range(CHUNKS):
        for q in range(4):
            s = 4 * j + q
            con[s] = (xt[pl.ds(off_ref[s], M), :] * window).astype(jnp.bfloat16)
        if j == 0:
            pl.semaphore_wait(barrier, 1 + 2 * (GROUP - 1) + (FAR - 1))
        for e in range(2):
            h = 2 * j + e
            remote(con.at[2 * h + 1 - core], theirs.at[h], core_s.at[h], core_r.at[h], sib).start()

    def near_copy(j, k):
        to_chip, to_side = place_of(k)
        src = merged.at[2 * j + to_side, pl.ds(pl.multiple_of(16 * to_chip, 16), 16)]
        return remote(src, near.at[j, k], near_s.at[j], near_r.at[j], partner(k, 0))

    for j in range(CHUNKS):
        for e in range(2):
            h = 2 * j + e
            remote(con.at[2 * h + 1 - core], theirs.at[h], core_s.at[h], core_r.at[h], sib).wait_recv()
            merged[h] = (con[2 * h + core].astype(jnp.float32) + theirs[h].astype(jnp.float32)).astype(jnp.bfloat16)

        @pl.loop(0, GROUP - 1)
        def _(k):
            near_copy(j, k).start()

    coords.wait()
    steps = lax.broadcasted_iota(jnp.int32, (TS, 128), 0).astype(jnp.float32)

    @pl.loop(0, VB // 128)
    def _(block):
        lanes = pl.ds(pl.multiple_of(128 * block, 128), 128)
        later = pl.ds(pl.multiple_of(VB + 128 * block, 128), 128)
        for k in range(NB):
            cos, sin = turn_cos_sin(steps * coords_ref[0, k : k + 1, lanes])
            cos, sin = cos.astype(jnp.bfloat16), sin.astype(jnp.bfloat16)
            row_phase[k, 0:TS, lanes] = cos
            row_phase[k, TS : 2 * TS, lanes] = sin
            row_phase[k, 0:TS, later] = -sin
            row_phase[k, TS : 2 * TS, later] = cos
            cos, sin = turn_cos_sin(steps * coords_ref[1, k : k + 1, lanes])
            col_cos[k, :, lanes] = cos
            col_sin[k, :, lanes] = sin

    mine = pl.ds(pl.multiple_of(16 * chip, 16), 16)

    def far_copy(j, k):
        return remote(far.at[j, ring], far.at[j, ring], far_s.at[j], far_r.at[j], along(k))

    def final(j):
        return grid.at[4 * (2 * (2 * j + side) + core) + chip // 4, pl.ds(pl.multiple_of(16 * lax.rem(chip, 4), 16), 16)]

    def all_copy(j, k):
        return remote(final(j), final(j), all_s.at[j], all_r.at[j], partner(k, 0))

    def other_copy(j, where):
        return remote(final(j), final(j), oth_s.at[j], oth_r.at[j], where)

    def fwd_copy(j, e, half):
        at = grid.at[pl.ds(4 * (2 * (2 * j + e) + half), 4)]
        return remote(at, at, fwd_s.at[j, e], fwd_r.at[j, e], sib)

    def wait_for(buffer, sem):
        pltpu.make_async_copy(buffer, buffer, sem).wait()

    for j in range(CHUNKS):
        wait_for(near.at[j, pl.ds(0, GROUP - 1)], near_r.at[j])
        total = merged[2 * j + side, mine].astype(jnp.float32)
        for k in range(GROUP - 1):
            total = total + near[j, k].astype(jnp.float32)
        far[j, ring] = total.astype(jnp.bfloat16)

        @pl.loop(0, FAR - 1)
        def _(k):
            far_copy(j, k).start()

    scale = 1.0 / math.sqrt(512)
    for j in range(CHUNKS):
        wait_for(far.at[j, pl.ds(0, FAR - 1)], far_r.at[j])
        total = far[j, 0].astype(jnp.float32)
        for k in range(1, FAR):
            total = total + far[j, k].astype(jnp.float32)
        grid[4 * (2 * (2 * j + side) + core) + chip // 4, pl.ds(pl.multiple_of(16 * lax.rem(chip, 4), 16), 16)] = (
            total * scale
        ).astype(jnp.bfloat16)

        @pl.loop(0, GROUP - 1)
        def _(k):
            all_copy(j, k).start()
            if j in DIRECT:
                other_copy(j, partner(k, 1)).start()

        if j in DIRECT:
            other_copy(j, sib).start()

    for j in range(CHUNKS):
        wait_for(near.at[j, pl.ds(0, GROUP - 1)], all_r.at[j])
        if j not in DIRECT:
            for e in range(2):
                fwd_copy(j, e, core).start()

    for j in range(CHUNKS):
        if j in DIRECT:
            wait_for(grid.at[pl.ds(0, 8)], oth_r.at[j])
        else:
            for e in range(2):
                fwd_copy(j, e, 1 - core).wait_recv()

    owners.wait()
    tiles.wait()
    count = jnp.int32(0)
    place = [jnp.int32(0)] * CAP
    for s in range(S):
        hit = (own_ref[s] == z).astype(jnp.int32)
        for slot in range(CAP):
            place[slot] = place[slot] + jnp.where((hit == 1) & (count == slot), s, 0)
        count = count + hit
    for slot in range(CAP):
        picked = grid[pl.ds(4 * place[slot], 4)].reshape(M, 2 * ROWS).astype(jnp.float32)
        picked = jnp.where(count > slot, picked, 0.0)
        sub_ref[slot] = jnp.transpose(picked).astype(jnp.bfloat16)

    for k in range(NB):
        tile = grid[tile_ref[k]]
        half = jnp.dot(tile, row_phase[k], preferred_element_type=jnp.float32)
        re, im = half[:, :VB], half[:, VB:]
        cos, sin = col_cos[k], col_sin[k]
        vis_ref[0, pl.ds(k, 1)] = jnp.sum(re * cos + im * sin, axis=0, keepdims=True) * (1.0 / TS)
        vis_ref[1, pl.ds(k, 1)] = jnp.sum(im * cos - re * sin, axis=0, keepdims=True) * (1.0 / TS)

    for j in range(CHUNKS):
        for e in range(2):
            h = 2 * j + e
            remote(con.at[2 * h + 1 - core], theirs.at[h], core_s.at[h], core_r.at[h], sib).wait_send()
            if j not in DIRECT:
                fwd_copy(j, e, core).wait_send()
        if j in DIRECT:
            wait_for(grid.at[pl.ds(0, 8)], oth_s.at[j])
        wait_for(near.at[j, pl.ds(0, GROUP - 1)], near_s.at[j])
        wait_for(far.at[j, pl.ds(0, FAR - 1)], far_s.at[j])
        wait_for(near.at[j, pl.ds(0, GROUP - 1)], all_s.at[j])


def on_device(strips, facet_window, sub_offset, sub_owner, block_tile, vis_coords):
    vmem = pl.BlockSpec(memory_space=pltpu.VMEM)
    dma = pltpu.SemaphoreType.DMA
    bf16, f32 = jnp.bfloat16, jnp.float32
    subgrids, visibilities = pl.pallas_call(
        kernel,
        out_shape=(
            pltpu.VMEM((CAP, 2 * ROWS, M), bf16),
            pltpu.VMEM((2, NB, VB), f32),
        ),
        in_specs=[pl.BlockSpec(memory_space=pltpu.HBM)] * 8,
        out_specs=(vmem, vmem),
        scratch_shapes=[
            pltpu.SMEM((S,), jnp.int32),
            pltpu.SMEM((S,), jnp.int32),
            pltpu.SMEM((NB,), jnp.int32),
            pltpu.VMEM((2, ROWS, L), bf16),
            pltpu.VMEM((1, M), f32),
            pltpu.VMEM((2, NB, VB), f32),
            pltpu.VMEM((M, 2 * M), bf16),
            pltpu.VMEM((2, RADIX, M), f32),
            pltpu.VMEM((RADIX, 2 * ROWS, 2 * M), bf16),
            pltpu.VMEM((L + M, 2 * ROWS), f32),
            pltpu.VMEM((S, M, 2 * ROWS), bf16),
            pltpu.VMEM((S // 2, M, 2 * ROWS), bf16),
            pltpu.VMEM((S // 2, M, 2 * ROWS), bf16),
            pltpu.VMEM((CHUNKS, GROUP - 1, 16, 2 * ROWS), bf16),
            pltpu.VMEM((CHUNKS, FAR, 16, 2 * ROWS), bf16),
            pltpu.VMEM((4 * S, TS, 2 * ROWS), bf16),
            pltpu.VMEM((NB, 2 * TS, 2 * VB), bf16),
            pltpu.VMEM((NB, TS, VB), f32),
            pltpu.VMEM((NB, TS, VB), f32),
            dma((11,)),
            dma((S // 2,)), dma((S // 2,)),
            dma((CHUNKS,)), dma((CHUNKS,)),
            dma((CHUNKS,)), dma((CHUNKS,)),
            dma((CHUNKS,)), dma((CHUNKS,)),
            dma((CHUNKS, 2)), dma((CHUNKS, 2)),
            dma((CHUNKS,)), dma((CHUNKS,)),
        ],
        compiler_params=pltpu.CompilerParams(
            collective_id=0, has_side_effects=True, vmem_limit_bytes=60 * 2**20
        ),
        name="predict",
    )(
        sub_offset, sub_owner, block_tile, strips.reshape(2, ROWS, L), facet_window.reshape(1, M), vis_coords,
        jnp.asarray(dft_table()), jnp.asarray(twiddle_table()),
    )
    return subgrids.reshape(1, CAP, 2, ROWS, M), visibilities


def solution(mesh):
    placed = (
        P(None, "frow", "fcol", None, None),
        P("frow", "fcol", None),
        P(),
        P(),
        P(("frow", "fcol")),
        P(None, ("frow", "fcol"), None),
    )
    return jax.shard_map(
        on_device,
        mesh=mesh,
        in_specs=placed,
        out_specs=(P("frow", None, None, None, None), P(None, ("frow", "fcol"), None)),
        check_vma=False,
    )
```

```python
import math

import jax
import jax.numpy as jnp
import numpy as np
from jax import lax
from jax.experimental import pallas as pl
from jax.experimental.pallas import tpu as pltpu
from jax.sharding import PartitionSpec as P

MESH = pl.DeviceIdType.MESH
TS = 64
CAP = 2
ROWS = 64
M = 256
L = 4096
S = 12
RADIX = 16
NB = 4
VB = 512
CHUNKS = 3
GROUP = 32
FAR = 8
DIRECT = (2,)


def dft_table():
    index = np.arange(M)
    angle = 2.0 * np.pi * ((index[:, None] * index[None, :]) % M) / M
    return np.concatenate([np.cos(angle), np.sin(angle)], axis=1).astype(jnp.bfloat16)


def twiddle_table():
    angle = 2.0 * np.pi * np.arange(RADIX)[:, None] * np.arange(M)[None, :] / L
    return np.stack([np.cos(angle), np.sin(angle)]).astype(np.float32)


def half_turn_polynomials():
    nodes = 0.5 * np.cos(np.pi * (np.arange(400) + 0.5) / 800)
    square = nodes * nodes
    sine = np.polynomial.polynomial.polyfit(square, np.sin(np.pi * nodes) / nodes, 5)
    cosine = np.polynomial.polynomial.polyfit(square, np.cos(np.pi * nodes), 5)
    return [float(v) for v in sine], [float(v) for v in cosine]


SINE, COSINE = half_turn_polynomials()


def turn_cos_sin(turns):
    r = turns - jnp.floor(turns + 0.5)
    u = r * r
    s = jnp.full_like(u, SINE[-1])
    c = jnp.full_like(u, COSINE[-1])
    for a, b in zip(SINE[-2::-1], COSINE[-2::-1]):
        s = s * u + a
        c = c * u + b
    s = s * r
    twice = s + s
    return 1.0 - twice * s, twice * c


def times_root(re, im, power):
    power = power % 16
    if power == 0:
        return re, im
    if power == 4:
        return -im, re
    if power == 8:
        return -re, -im
    if power == 12:
        return im, -re
    c = math.cos(2.0 * math.pi * power / 16)
    s = math.sin(2.0 * math.pi * power / 16)
    if power in (2, 6, 10, 14):
        a = abs(c)
        plus, minus = (re + im) * a, (re - im) * a
        return {2: (minus, plus), 6: (-plus, minus), 10: (-minus, -plus), 14: (plus, -minus)}[power]
    return re * c - im * s, re * s + im * c


def dft4(v):
    (ar, ai), (br, bi), (cr, ci), (dr, di) = v
    pr, pi_, qr, qi = ar + cr, ai + ci, ar - cr, ai - ci
    sr, si, tr, ti = br + dr, bi + di, br - dr, bi - di
    return [(pr + sr, pi_ + si), (qr - ti, qi + tr), (pr - sr, pi_ - si), (qr + ti, qi - tr)]


def dft16(x):
    inner = []
    for low in range(4):
        inner.append(dft4([x[4 * high + low] for high in range(4)]))
    out = [None] * 16
    for c0 in range(4):
        column = [times_root(*inner[low][c0], low * c0) for low in range(4)]
        for c1, value in enumerate(dft4(column)):
            out[4 * c1 + c0] = value
    return out


def steps_of(step):
    dx, dy, dz = step
    return min(dx, 4 - dx) + min(dy, 4 - dy) + dz


ORDER = sorted(((dx, dy, dz) for dx in range(4) for dy in range(4) for dz in range(2)), key=steps_of, reverse=True)


def kernel(
    off_hbm, own_hbm, tile_hbm, strips_hbm, window_hbm, coords_hbm, table_hbm, twiddle_hbm,
    sub_ref, vis_ref,
    off_ref, own_ref, tile_ref, strips, window_ref, coords_ref, table_ref, twiddle_ref, zb, xt, con, theirs, merged, near, far, grid, row_phase, col_cos, col_sin,
    load_sem, core_s, core_r, near_s, near_r, far_s, far_r, all_s, all_r, fwd_s, fwd_r, oth_s, oth_r,
):
    z = lax.axis_index("frow")
    f = lax.axis_index("fcol")
    core = lax.rem(f, 2)
    chip = f // 2
    x, y = chip // 4, lax.rem(chip, 4)
    side = lax.rem(z, 2)
    ring = z // 2
    sibling = f + 1 - 2 * core

    def loads(part):
        rows = pl.ds(16 * part, 16)
        return pltpu.make_async_copy(strips_hbm.at[:, rows], strips.at[:, rows], load_sem.at[part])

    def whole(src, dst, n):
        return pltpu.make_async_copy(src, dst, load_sem.at[4 + n])

    twiddles = whole(twiddle_hbm, twiddle_ref, 0)
    table = whole(table_hbm, table_ref, 1)
    windows = whole(window_hbm, window_ref, 2)
    coords = whole(coords_hbm, coords_ref, 3)
    offsets = whole(off_hbm, off_ref, 4)
    owners = whole(own_hbm, own_ref, 5)
    tiles = whole(tile_hbm, tile_ref, 6)
    loads(0).start()
    twiddles.start()
    for part in range(1, 4):
        loads(part).start()
    table.start()

    xs = [x] + [lax.rem(x + d, 4) for d in range(1, 4)]
    ys = [y] + [lax.rem(y + d, 4) for d in range(1, 4)]
    chips = [[4 * xs[a] + ys[b] for b in range(4)] for a in range(4)]
    sides = [side, 1 - side]
    rows_of = [[pl.ds(pl.multiple_of(16 * chips[a][b], 16), 16) for b in range(4)] for a in range(4)]
    frows = [z, 2 * ring + 1 - side]
    fcols = [[[2 * chips[a][b] + core, 2 * chips[a][b] + 1 - core] for b in range(4)] for a in range(4)]

    def partner(k, other):
        dx, dy, dz = ORDER[k]
        return {"frow": frows[dz], "fcol": fcols[dx][dy][other]}

    def along(k):
        step = (4, 3, 5, 2, 6, 1, 7)[k]
        return {"frow": 2 * lax.rem(ring + step, FAR) + side, "fcol": f}

    sib = {"frow": z, "fcol": sibling}
    barrier = pltpu.get_barrier_semaphore()

    for k in range(FAR - 1):
        pl.semaphore_signal(barrier, inc=1, device_id=along(k), device_id_type=MESH)

    for k in range(GROUP - 1):
        pl.semaphore_signal(barrier, inc=1, device_id=partner(k, 0), device_id_type=MESH)
        pl.semaphore_signal(barrier, inc=1, device_id=partner(k, 1), device_id_type=MESH)

    pl.semaphore_signal(barrier, inc=1, device_id=sib, device_id_type=MESH)
    for load in (offsets, windows, coords, owners, tiles):
        load.start()

    def remote(src, dst, send, recv, where):
        return pltpu.make_async_remote_copy(
            src_ref=src, dst_ref=dst, send_sem=send, recv_sem=recv, device_id=where, device_id_type=MESH
        )

    twiddles.wait()
    for part in range(4):
        loads(part).wait()
        rows = pl.ds(16 * part, 16)
        low_rows = pl.ds(ROWS + 16 * part, 16)

        @pl.loop(0, 2)
        def _(half):
            lane = pl.multiple_of(half * 128, 128)
            samples = []
            for g in range(RADIX):
                lanes = pl.ds(pl.multiple_of(M * g + lane, 128), 128)
                samples.append((strips[0, rows, lanes].astype(jnp.float32), strips[1, rows, lanes].astype(jnp.float32)))
            first = pl.ds(lane, 128)
            second = pl.ds(pl.multiple_of(M + lane, 128), 128)
            for c, (re, im) in enumerate(dft16(samples)):
                if c:
                    cos = twiddle_ref[0, pl.ds(c, 1), first]
                    sin = twiddle_ref[1, pl.ds(c, 1), first]
                    re, im = re * cos - im * sin, re * sin + im * cos
                re16, im16 = re.astype(jnp.bfloat16), im.astype(jnp.bfloat16)
                zb[c, rows, first] = re16
                zb[c, rows, second] = -im16
                zb[c, low_rows, first] = im16
                zb[c, low_rows, second] = re16

    table.wait()
    for pair in range(RADIX // 2):
        both = zb[2 * pair : 2 * pair + 2].reshape(2 * 128, 2 * M)
        product = lax.dot_general(
            table_ref[...], both, (((1,), (1,)), ((), ())), preferred_element_type=jnp.float32
        )
        for e in range(2):
            c = 2 * pair + e
            piece = product[:, 128 * e : 128 * e + 128]
            xt[pl.ds(c, M, stride=RADIX), :] = piece
            xt[pl.ds(L + c, M // RADIX, stride=RADIX), :] = piece[: M // RADIX]

    windows.wait()
    offsets.wait()
    window = jnp.transpose(jnp.broadcast_to(window_ref[...], (128, M)))

    for j in range(CHUNKS):
        for q in range(4):
            s = 4 * j + q
            con[s] = (xt[pl.ds(off_ref[s], M), :] * window).astype(jnp.bfloat16)
        if j == 0:
            pl.semaphore_wait(barrier, 1 + 2 * (GROUP - 1) + (FAR - 1))
        for e in range(2):
            h = 2 * j + e
            remote(con.at[2 * h + 1 - core], theirs.at[h], core_s.at[h], core_r.at[h], sib).start()

    def near_copy(j, k):
        dx, dy, dz = ORDER[k]
        src = merged.at[2 * j + sides[dz], rows_of[dx][dy]]
        return remote(src, near.at[j, k], near_s.at[j], near_r.at[j], partner(k, 0))

    for j in range(CHUNKS):
        for e in range(2):
            h = 2 * j + e
            remote(con.at[2 * h + 1 - core], theirs.at[h], core_s.at[h], core_r.at[h], sib).wait_recv()
            merged[h] = (con[2 * h + core].astype(jnp.float32) + theirs[h].astype(jnp.float32)).astype(jnp.bfloat16)

        for k in range(GROUP - 1):
            near_copy(j, k).start()

    coords.wait()
    steps = lax.broadcasted_iota(jnp.int32, (TS, 128), 0).astype(jnp.float32)

    @pl.loop(0, VB // 128)
    def _(block):
        lanes = pl.ds(pl.multiple_of(128 * block, 128), 128)
        later = pl.ds(pl.multiple_of(VB + 128 * block, 128), 128)
        for k in range(NB):
            cos, sin = turn_cos_sin(steps * coords_ref[0, k : k + 1, lanes])
            cos, sin = cos.astype(jnp.bfloat16), sin.astype(jnp.bfloat16)
            row_phase[k, 0:TS, lanes] = cos
            row_phase[k, TS : 2 * TS, lanes] = sin
            row_phase[k, 0:TS, later] = -sin
            row_phase[k, TS : 2 * TS, later] = cos
            cos, sin = turn_cos_sin(steps * coords_ref[1, k : k + 1, lanes])
            col_cos[k, :, lanes] = cos
            col_sin[k, :, lanes] = sin

    mine = pl.ds(pl.multiple_of(16 * chip, 16), 16)

    def far_copy(j, k):
        return remote(far.at[j, ring], far.at[j, ring], far_s.at[j], far_r.at[j], along(k))

    def final(j):
        return grid.at[4 * (2 * (2 * j + side) + core) + chip // 4, pl.ds(pl.multiple_of(16 * lax.rem(chip, 4), 16), 16)]

    def all_copy(j, k):
        return remote(final(j), final(j), all_s.at[j], all_r.at[j], partner(k, 0))

    def other_copy(j, where):
        return remote(final(j), final(j), oth_s.at[j], oth_r.at[j], where)

    def fwd_copy(j, e, half):
        at = grid.at[pl.ds(4 * (2 * (2 * j + e) + half), 4)]
        return remote(at, at, fwd_s.at[j, e], fwd_r.at[j, e], sib)

    def wait_for(buffer, sem):
        pltpu.make_async_copy(buffer, buffer, sem).wait()

    for j in range(CHUNKS):
        wait_for(near.at[j, pl.ds(0, GROUP - 1)], near_r.at[j])
        total = merged[2 * j + side, mine].astype(jnp.float32)
        for k in range(GROUP - 1):
            total = total + near[j, k].astype(jnp.float32)
        far[j, ring] = total.astype(jnp.bfloat16)

        for k in range(FAR - 1):
            far_copy(j, k).start()

    scale = 1.0 / math.sqrt(512)
    for j in range(CHUNKS):
        wait_for(far.at[j, pl.ds(0, FAR - 1)], far_r.at[j])
        total = far[j, 0].astype(jnp.float32)
        for k in range(1, FAR):
            total = total + far[j, k].astype(jnp.float32)
        grid[4 * (2 * (2 * j + side) + core) + chip // 4, pl.ds(pl.multiple_of(16 * lax.rem(chip, 4), 16), 16)] = (
            total * scale
        ).astype(jnp.bfloat16)

        for k in range(GROUP - 1):
            all_copy(j, k).start()
            if j in DIRECT:
                other_copy(j, partner(k, 1)).start()

        if j in DIRECT:
            other_copy(j, sib).start()

    for j in range(CHUNKS):
        wait_for(near.at[j, pl.ds(0, GROUP - 1)], all_r.at[j])
        if j not in DIRECT:
            for e in range(2):
                fwd_copy(j, e, core).start()

    for j in range(CHUNKS):
        if j in DIRECT:
            wait_for(grid.at[pl.ds(0, 8)], oth_r.at[j])
        else:
            for e in range(2):
                fwd_copy(j, e, 1 - core).wait_recv()

    owners.wait()
    tiles.wait()
    count = jnp.int32(0)
    place = [jnp.int32(0)] * CAP
    for s in range(S):
        hit = (own_ref[s] == z).astype(jnp.int32)
        for slot in range(CAP):
            place[slot] = place[slot] + jnp.where((hit == 1) & (count == slot), s, 0)
        count = count + hit
    for slot in range(CAP):
        picked = grid[pl.ds(4 * place[slot], 4)].reshape(M, 2 * ROWS).astype(jnp.float32)
        picked = jnp.where(count > slot, picked, 0.0)
        sub_ref[slot] = jnp.transpose(picked).astype(jnp.bfloat16)

    for k in range(NB):
        tile = grid[tile_ref[k]]
        half = jnp.dot(tile, row_phase[k], preferred_element_type=jnp.float32)
        re, im = half[:, :VB], half[:, VB:]
        cos, sin = col_cos[k], col_sin[k]
        vis_ref[0, pl.ds(k, 1)] = jnp.sum(re * cos + im * sin, axis=0, keepdims=True) * (1.0 / TS)
        vis_ref[1, pl.ds(k, 1)] = jnp.sum(im * cos - re * sin, axis=0, keepdims=True) * (1.0 / TS)

    for j in range(CHUNKS):
        for e in range(2):
            h = 2 * j + e
            remote(con.at[2 * h + 1 - core], theirs.at[h], core_s.at[h], core_r.at[h], sib).wait_send()
            if j not in DIRECT:
                fwd_copy(j, e, core).wait_send()
        if j in DIRECT:
            wait_for(grid.at[pl.ds(0, 8)], oth_s.at[j])
        wait_for(near.at[j, pl.ds(0, GROUP - 1)], near_s.at[j])
        wait_for(far.at[j, pl.ds(0, FAR - 1)], far_s.at[j])
        wait_for(near.at[j, pl.ds(0, GROUP - 1)], all_s.at[j])


def on_device(strips, facet_window, sub_offset, sub_owner, block_tile, vis_coords):
    vmem = pl.BlockSpec(memory_space=pltpu.VMEM)
    dma = pltpu.SemaphoreType.DMA
    bf16, f32 = jnp.bfloat16, jnp.float32
    subgrids, visibilities = pl.pallas_call(
        kernel,
        out_shape=(
            pltpu.VMEM((CAP, 2 * ROWS, M), bf16),
            pltpu.VMEM((2, NB, VB), f32),
        ),
        in_specs=[pl.BlockSpec(memory_space=pltpu.HBM)] * 8,
        out_specs=(vmem, vmem),
        scratch_shapes=[
            pltpu.SMEM((S,), jnp.int32),
            pltpu.SMEM((S,), jnp.int32),
            pltpu.SMEM((NB,), jnp.int32),
            pltpu.VMEM((2, ROWS, L), bf16),
            pltpu.VMEM((1, M), f32),
            pltpu.VMEM((2, NB, VB), f32),
            pltpu.VMEM((M, 2 * M), bf16),
            pltpu.VMEM((2, RADIX, M), f32),
            pltpu.VMEM((RADIX, 2 * ROWS, 2 * M), bf16),
            pltpu.VMEM((L + M, 2 * ROWS), f32),
            pltpu.VMEM((S, M, 2 * ROWS), bf16),
            pltpu.VMEM((S // 2, M, 2 * ROWS), bf16),
            pltpu.VMEM((S // 2, M, 2 * ROWS), bf16),
            pltpu.VMEM((CHUNKS, GROUP - 1, 16, 2 * ROWS), bf16),
            pltpu.VMEM((CHUNKS, FAR, 16, 2 * ROWS), bf16),
            pltpu.VMEM((4 * S, TS, 2 * ROWS), bf16),
            pltpu.VMEM((NB, 2 * TS, 2 * VB), bf16),
            pltpu.VMEM((NB, TS, VB), f32),
            pltpu.VMEM((NB, TS, VB), f32),
            dma((11,)),
            dma((S // 2,)), dma((S // 2,)),
            dma((CHUNKS,)), dma((CHUNKS,)),
            dma((CHUNKS,)), dma((CHUNKS,)),
            dma((CHUNKS,)), dma((CHUNKS,)),
            dma((CHUNKS, 2)), dma((CHUNKS, 2)),
            dma((CHUNKS,)), dma((CHUNKS,)),
        ],
        compiler_params=pltpu.CompilerParams(
            collective_id=0, has_side_effects=True, vmem_limit_bytes=60 * 2**20
        ),
        name="predict",
    )(
        sub_offset, sub_owner, block_tile, strips.reshape(2, ROWS, L), facet_window.reshape(1, M), vis_coords,
        jnp.asarray(dft_table()), jnp.asarray(twiddle_table()),
    )
    return subgrids.reshape(1, CAP, 2, ROWS, M), visibilities


def solution(mesh):
    placed = (
        P(None, "frow", "fcol", None, None),
        P("frow", "fcol", None),
        P(),
        P(),
        P(("frow", "fcol")),
        P(None, ("frow", "fcol"), None),
    )
    return jax.shard_map(
        on_device,
        mesh=mesh,
        in_specs=placed,
        out_specs=(P("frow", None, None, None, None), P(None, ("frow", "fcol"), None)),
        check_vma=False,
    )
```

```python
import math

import jax
import jax.numpy as jnp
import numpy as np
from jax import lax
from jax.experimental import pallas as pl
from jax.experimental.pallas import tpu as pltpu
from jax.sharding import PartitionSpec as P

MESH = pl.DeviceIdType.MESH
TS = 64
CAP = 2
ROWS = 64
M = 256
L = 4096
S = 12
RADIX = 16
NB = 4
VB = 512
CHUNKS = 3
GROUP = 32
FAR = 8
DIRECT = (2,)


def dft_table():
    index = np.arange(M)
    angle = 2.0 * np.pi * ((index[:, None] * index[None, :]) % M) / M
    return np.concatenate([np.cos(angle), np.sin(angle)], axis=1).astype(jnp.bfloat16)


def twiddle_table():
    angle = 2.0 * np.pi * np.arange(RADIX)[:, None] * np.arange(M)[None, :] / L
    return np.stack([np.cos(angle), np.sin(angle)]).astype(np.float32)


def half_turn_polynomials():
    nodes = 0.5 * np.cos(np.pi * (np.arange(400) + 0.5) / 800)
    square = nodes * nodes
    sine = np.polynomial.polynomial.polyfit(square, np.sin(np.pi * nodes) / nodes, 5)
    cosine = np.polynomial.polynomial.polyfit(square, np.cos(np.pi * nodes), 5)
    return [float(v) for v in sine], [float(v) for v in cosine]


SINE, COSINE = half_turn_polynomials()


def turn_cos_sin(turns):
    r = turns - jnp.floor(turns + 0.5)
    u = r * r
    s = jnp.full_like(u, SINE[-1])
    c = jnp.full_like(u, COSINE[-1])
    for a, b in zip(SINE[-2::-1], COSINE[-2::-1]):
        s = s * u + a
        c = c * u + b
    s = s * r
    twice = s + s
    return 1.0 - twice * s, twice * c


def times_root(re, im, power):
    power = power % 16
    if power == 0:
        return re, im
    if power == 4:
        return -im, re
    if power == 8:
        return -re, -im
    if power == 12:
        return im, -re
    c = math.cos(2.0 * math.pi * power / 16)
    s = math.sin(2.0 * math.pi * power / 16)
    if power in (2, 6, 10, 14):
        a = abs(c)
        plus, minus = (re + im) * a, (re - im) * a
        return {2: (minus, plus), 6: (-plus, minus), 10: (-minus, -plus), 14: (plus, -minus)}[power]
    return re * c - im * s, re * s + im * c


def dft4(v):
    (ar, ai), (br, bi), (cr, ci), (dr, di) = v
    pr, pi_, qr, qi = ar + cr, ai + ci, ar - cr, ai - ci
    sr, si, tr, ti = br + dr, bi + di, br - dr, bi - di
    return [(pr + sr, pi_ + si), (qr - ti, qi + tr), (pr - sr, pi_ - si), (qr + ti, qi - tr)]


def dft16(x):
    inner = []
    for low in range(4):
        inner.append(dft4([x[4 * high + low] for high in range(4)]))
    out = [None] * 16
    for c0 in range(4):
        column = [times_root(*inner[low][c0], low * c0) for low in range(4)]
        for c1, value in enumerate(dft4(column)):
            out[4 * c1 + c0] = value
    return out


def steps_of(step):
    dx, dy, dz = step
    return min(dx, 4 - dx) + min(dy, 4 - dy) + dz


ORDER = sorted(((dx, dy, dz) for dx in range(4) for dy in range(4) for dz in range(2)), key=steps_of, reverse=True)


def kernel(
    off_hbm, own_hbm, tile_hbm, strips_hbm, window_hbm, coords_hbm, table_hbm, twiddle_hbm,
    sub_ref, vis_ref,
    off_ref, own_ref, tile_ref, strips, window_ref, coords_ref, table_ref, twiddle_ref, zb, xt, con, theirs, merged, near, far, grid, row_phase, col_cos, col_sin,
    load_sem, core_s, core_r, near_s, near_r, far_s, far_r, all_s, all_r, fwd_s, fwd_r, oth_s, oth_r,
):
    z = lax.axis_index("frow")
    f = lax.axis_index("fcol")
    core = lax.rem(f, 2)
    chip = f // 2
    x, y = chip // 4, lax.rem(chip, 4)
    side = lax.rem(z, 2)
    ring = z // 2
    sibling = f + 1 - 2 * core

    def loads(part):
        rows = pl.ds(16 * part, 16)
        return pltpu.make_async_copy(strips_hbm.at[:, rows], strips.at[:, rows], load_sem.at[part])

    def whole(src, dst, n):
        return pltpu.make_async_copy(src, dst, load_sem.at[4 + n])

    twiddles = whole(twiddle_hbm, twiddle_ref, 0)
    table = whole(table_hbm, table_ref, 1)
    windows = whole(window_hbm, window_ref, 2)
    coords = whole(coords_hbm, coords_ref, 3)
    offsets = whole(off_hbm, off_ref, 4)
    owners = whole(own_hbm, own_ref, 5)
    tiles = whole(tile_hbm, tile_ref, 6)
    loads(0).start()
    twiddles.start()
    for part in range(1, 4):
        loads(part).start()
    table.start()

    xs = [x] + [lax.rem(x + d, 4) for d in range(1, 4)]
    ys = [y] + [lax.rem(y + d, 4) for d in range(1, 4)]
    chips = [[4 * xs[a] + ys[b] for b in range(4)] for a in range(4)]
    sides = [side, 1 - side]
    rows_of = [[pl.ds(pl.multiple_of(16 * chips[a][b], 16), 16) for b in range(4)] for a in range(4)]
    frows = [z, 2 * ring + 1 - side]
    fcols = [[[2 * chips[a][b] + core, 2 * chips[a][b] + 1 - core] for b in range(4)] for a in range(4)]

    def partner(k, other):
        dx, dy, dz = ORDER[k]
        return {"frow": frows[dz], "fcol": fcols[dx][dy][other]}

    def along(k):
        step = (4, 3, 5, 2, 6, 1, 7)[k]
        return {"frow": 2 * lax.rem(ring + step, FAR) + side, "fcol": f}

    sib = {"frow": z, "fcol": sibling}
    barrier = pltpu.get_barrier_semaphore()

    for k in range(FAR - 1):
        pl.semaphore_signal(barrier, inc=1, device_id=along(k), device_id_type=MESH)

    for k in range(GROUP - 1):
        pl.semaphore_signal(barrier, inc=1, device_id=partner(k, 0), device_id_type=MESH)
        pl.semaphore_signal(barrier, inc=1, device_id=partner(k, 1), device_id_type=MESH)

    pl.semaphore_signal(barrier, inc=1, device_id=sib, device_id_type=MESH)
    for load in (offsets, windows, coords, owners, tiles):
        load.start()

    def remote(src, dst, send, recv, where):
        return pltpu.make_async_remote_copy(
            src_ref=src, dst_ref=dst, send_sem=send, recv_sem=recv, device_id=where, device_id_type=MESH
        )

    twiddles.wait()
    for part in range(4):
        loads(part).wait()
        rows = pl.ds(16 * part, 16)
        low_rows = pl.ds(ROWS + 16 * part, 16)

        @pl.loop(0, 2)
        def _(half):
            lane = pl.multiple_of(half * 128, 128)
            samples = []
            for g in range(RADIX):
                lanes = pl.ds(pl.multiple_of(M * g + lane, 128), 128)
                samples.append((strips[0, rows, lanes].astype(jnp.float32), strips[1, rows, lanes].astype(jnp.float32)))
            first = pl.ds(lane, 128)
            second = pl.ds(pl.multiple_of(M + lane, 128), 128)
            for c, (re, im) in enumerate(dft16(samples)):
                if c:
                    cos = twiddle_ref[0, pl.ds(c, 1), first]
                    sin = twiddle_ref[1, pl.ds(c, 1), first]
                    re, im = re * cos - im * sin, re * sin + im * cos
                re16, im16 = re.astype(jnp.bfloat16), im.astype(jnp.bfloat16)
                zb[c, rows, first] = re16
                zb[c, rows, second] = -im16
                zb[c, low_rows, first] = im16
                zb[c, low_rows, second] = re16

    table.wait()
    for pair in range(RADIX // 2):
        both = zb[2 * pair : 2 * pair + 2].reshape(2 * 128, 2 * M)
        product = lax.dot_general(
            table_ref[...], both, (((1,), (1,)), ((), ())), preferred_element_type=jnp.float32
        )
        for e in range(2):
            c = 2 * pair + e
            piece = product[:, 128 * e : 128 * e + 128]
            xt[pl.ds(c, M, stride=RADIX), :] = piece
            xt[pl.ds(L + c, M // RADIX, stride=RADIX), :] = piece[: M // RADIX]

    windows.wait()
    offsets.wait()
    window = jnp.transpose(jnp.broadcast_to(window_ref[...], (128, M)))

    for j in range(CHUNKS):
        for q in range(4):
            s = 4 * j + q
            con[s] = (xt[pl.ds(off_ref[s], M), :] * window).astype(jnp.bfloat16)
        if j == 0:
            pl.semaphore_wait(barrier, 1 + 2 * (GROUP - 1) + (FAR - 1))
        for e in range(2):
            h = 2 * j + e
            remote(con.at[2 * h + 1 - core], theirs.at[h], core_s.at[h], core_r.at[h], sib).start()

    def near_copy(j, k):
        dx, dy, dz = ORDER[k]
        src = merged.at[2 * j + sides[dz], rows_of[dx][dy]]
        return remote(src, near.at[j, k], near_s.at[j], near_r.at[j], partner(k, 0))

    for j in range(CHUNKS):
        for e in range(2):
            h = 2 * j + e
            remote(con.at[2 * h + 1 - core], theirs.at[h], core_s.at[h], core_r.at[h], sib).wait_recv()
            merged[h] = (con[2 * h + core].astype(jnp.float32) + theirs[h].astype(jnp.float32)).astype(jnp.bfloat16)

        for k in range(GROUP - 1):
            near_copy(j, k).start()

    coords.wait()
    steps = lax.broadcasted_iota(jnp.int32, (TS, 128), 0).astype(jnp.float32)

    @pl.loop(0, VB // 128)
    def _(block):
        lanes = pl.ds(pl.multiple_of(128 * block, 128), 128)
        later = pl.ds(pl.multiple_of(VB + 128 * block, 128), 128)
        for k in range(NB):
            cos, sin = turn_cos_sin(steps * coords_ref[0, k : k + 1, lanes])
            cos, sin = cos.astype(jnp.bfloat16), sin.astype(jnp.bfloat16)
            row_phase[k, 0:TS, lanes] = cos
            row_phase[k, TS : 2 * TS, lanes] = sin
            row_phase[k, 0:TS, later] = -sin
            row_phase[k, TS : 2 * TS, later] = cos
            cos, sin = turn_cos_sin(steps * coords_ref[1, k : k + 1, lanes])
            col_cos[k, :, lanes] = cos
            col_sin[k, :, lanes] = sin

    mine = pl.ds(pl.multiple_of(16 * chip, 16), 16)

    def far_copy(j, k):
        return remote(far.at[j, ring], far.at[j, ring], far_s.at[j], far_r.at[j], along(k))

    def final(j):
        return grid.at[4 * (2 * (2 * j + side) + core) + chip // 4, pl.ds(pl.multiple_of(16 * lax.rem(chip, 4), 16), 16)]

    def all_copy(j, k):
        return remote(final(j), final(j), all_s.at[j], all_r.at[j], partner(k, 0))

    def other_copy(j, where):
        return remote(final(j), final(j), oth_s.at[j], oth_r.at[j], where)

    def fwd_copy(j, e, half):
        at = grid.at[pl.ds(4 * (2 * (2 * j + e) + half), 4)]
        return remote(at, at, fwd_s.at[j, e], fwd_r.at[j, e], sib)

    def wait_for(buffer, sem):
        pltpu.make_async_copy(buffer, buffer, sem).wait()

    for j in range(CHUNKS):
        wait_for(near.at[j, pl.ds(0, GROUP - 1)], near_r.at[j])
        total = merged[2 * j + side, mine].astype(jnp.float32)
        for k in range(GROUP - 1):
            total = total + near[j, k].astype(jnp.float32)
        far[j, ring] = total.astype(jnp.bfloat16)

        for k in range(FAR - 1):
            far_copy(j, k).start()

    scale = 1.0 / math.sqrt(512)
    for j in range(CHUNKS):
        wait_for(far.at[j, pl.ds(0, FAR - 1)], far_r.at[j])
        total = far[j, 0].astype(jnp.float32)
        for k in range(1, FAR):
            total = total + far[j, k].astype(jnp.float32)
        grid[4 * (2 * (2 * j + side) + core) + chip // 4, pl.ds(pl.multiple_of(16 * lax.rem(chip, 4), 16), 16)] = (
            total * scale
        ).astype(jnp.bfloat16)

        for k in range(GROUP - 1):
            all_copy(j, k).start()
            if j in DIRECT:
                other_copy(j, partner(k, 1)).start()

        if j in DIRECT:
            other_copy(j, sib).start()

    for j in range(CHUNKS):
        wait_for(near.at[j, pl.ds(0, GROUP - 1)], all_r.at[j])
        if j not in DIRECT:
            for e in range(2):
                fwd_copy(j, e, core).start()

    for j in range(CHUNKS):
        if j in DIRECT:
            wait_for(grid.at[pl.ds(0, 8)], oth_r.at[j])
        else:
            for e in range(2):
                fwd_copy(j, e, 1 - core).wait_recv()

    owners.wait()
    tiles.wait()
    count = jnp.int32(0)
    place = [jnp.int32(0)] * CAP
    for s in range(S):
        hit = (own_ref[s] == z).astype(jnp.int32)
        for slot in range(CAP):
            place[slot] = place[slot] + jnp.where((hit == 1) & (count == slot), s, 0)
        count = count + hit
    for slot in range(CAP):
        picked = grid[pl.ds(4 * place[slot], 4)].reshape(M, 2 * ROWS).astype(jnp.float32)
        picked = jnp.where(count > slot, picked, 0.0)
        sub_ref[slot] = jnp.transpose(picked).astype(jnp.bfloat16)

    for k in range(NB):
        tile = grid[tile_ref[k]]
        half = jnp.dot(tile, row_phase[k], preferred_element_type=jnp.float32)
        re, im = half[:, :VB], half[:, VB:]
        cos, sin = col_cos[k], col_sin[k]
        vis_ref[0, pl.ds(k, 1)] = jnp.sum(re * cos + im * sin, axis=0, keepdims=True) * (1.0 / TS)
        vis_ref[1, pl.ds(k, 1)] = jnp.sum(im * cos - re * sin, axis=0, keepdims=True) * (1.0 / TS)

    for j in range(CHUNKS):
        for e in range(2):
            h = 2 * j + e
            remote(con.at[2 * h + 1 - core], theirs.at[h], core_s.at[h], core_r.at[h], sib).wait_send()
            if j not in DIRECT:
                fwd_copy(j, e, core).wait_send()
        if j in DIRECT:
            wait_for(grid.at[pl.ds(0, 8)], oth_s.at[j])
        wait_for(near.at[j, pl.ds(0, GROUP - 1)], near_s.at[j])
        wait_for(far.at[j, pl.ds(0, FAR - 1)], far_s.at[j])
        wait_for(near.at[j, pl.ds(0, GROUP - 1)], all_s.at[j])


def write_out(sub_ref, vis_ref, sub_hbm, vis_hbm, sems):
    copies = [
        pltpu.make_async_copy(sub_ref, sub_hbm, sems.at[0]),
        pltpu.make_async_copy(vis_ref, vis_hbm, sems.at[1]),
    ]
    for copy in copies:
        copy.start()
    for copy in copies:
        copy.wait()


def on_device(strips, facet_window, sub_offset, sub_owner, block_tile, vis_coords):
    vmem = pl.BlockSpec(memory_space=pltpu.VMEM)
    dma = pltpu.SemaphoreType.DMA
    bf16, f32 = jnp.bfloat16, jnp.float32
    subgrids, visibilities = pl.pallas_call(
        kernel,
        out_shape=(
            pltpu.VMEM((CAP, 2 * ROWS, M), bf16),
            pltpu.VMEM((2, NB, VB), f32),
        ),
        in_specs=[pl.BlockSpec(memory_space=pltpu.HBM)] * 8,
        out_specs=(vmem, vmem),
        scratch_shapes=[
            pltpu.SMEM((S,), jnp.int32),
            pltpu.SMEM((S,), jnp.int32),
            pltpu.SMEM((NB,), jnp.int32),
            pltpu.VMEM((2, ROWS, L), bf16),
            pltpu.VMEM((1, M), f32),
            pltpu.VMEM((2, NB, VB), f32),
            pltpu.VMEM((M, 2 * M), bf16),
            pltpu.VMEM((2, RADIX, M), f32),
            pltpu.VMEM((RADIX, 2 * ROWS, 2 * M), bf16),
            pltpu.VMEM((L + M, 2 * ROWS), f32),
            pltpu.VMEM((S, M, 2 * ROWS), bf16),
            pltpu.VMEM((S // 2, M, 2 * ROWS), bf16),
            pltpu.VMEM((S // 2, M, 2 * ROWS), bf16),
            pltpu.VMEM((CHUNKS, GROUP - 1, 16, 2 * ROWS), bf16),
            pltpu.VMEM((CHUNKS, FAR, 16, 2 * ROWS), bf16),
            pltpu.VMEM((4 * S, TS, 2 * ROWS), bf16),
            pltpu.VMEM((NB, 2 * TS, 2 * VB), bf16),
            pltpu.VMEM((NB, TS, VB), f32),
            pltpu.VMEM((NB, TS, VB), f32),
            dma((11,)),
            dma((S // 2,)), dma((S // 2,)),
            dma((CHUNKS,)), dma((CHUNKS,)),
            dma((CHUNKS,)), dma((CHUNKS,)),
            dma((CHUNKS,)), dma((CHUNKS,)),
            dma((CHUNKS, 2)), dma((CHUNKS, 2)),
            dma((CHUNKS,)), dma((CHUNKS,)),
        ],
        compiler_params=pltpu.CompilerParams(
            collective_id=0, has_side_effects=True, vmem_limit_bytes=60 * 2**20
        ),
        name="predict",
    )(
        sub_offset, sub_owner, block_tile, strips.reshape(2, ROWS, L), facet_window.reshape(1, M), vis_coords,
        jnp.asarray(dft_table()), jnp.asarray(twiddle_table()),
    )
    subgrids, visibilities = pl.pallas_call(
        write_out,
        out_shape=(
            jax.ShapeDtypeStruct((CAP, 2 * ROWS, M), bf16),
            jax.ShapeDtypeStruct((2, NB, VB), f32),
        ),
        in_specs=[vmem, vmem],
        out_specs=(pl.BlockSpec(memory_space=pltpu.HBM), pl.BlockSpec(memory_space=pltpu.HBM)),
        scratch_shapes=[dma((2,))],
        compiler_params=pltpu.CompilerParams(vmem_limit_bytes=2**20),
        name="write_out",
    )(subgrids, visibilities)
    return subgrids.reshape(1, CAP, 2, ROWS, M), visibilities


def solution(mesh):
    placed = (
        P(None, "frow", "fcol", None, None),
        P("frow", "fcol", None),
        P(),
        P(),
        P(("frow", "fcol")),
        P(None, ("frow", "fcol"), None),
    )
    return jax.shard_map(
        on_device,
        mesh=mesh,
        in_specs=placed,
        out_specs=(P("frow", None, None, None, None), P(None, ("frow", "fcol"), None)),
        check_vma=False,
    )
```

```python
import math

import jax
import jax.numpy as jnp
import numpy as np
from jax import lax
from jax.experimental import pallas as pl
from jax.experimental.pallas import tpu as pltpu
from jax.sharding import PartitionSpec as P

MESH = pl.DeviceIdType.MESH
TS = 64
CAP = 2
ROWS = 64
M = 256
L = 4096
S = 12
RADIX = 16
NB = 4
VB = 512
CHUNKS = 3
GROUP = 32
FAR = 8
DIRECT = (2,)


def dft_table():
    index = np.arange(M)
    angle = 2.0 * np.pi * ((index[:, None] * index[None, :]) % M) / M
    return np.concatenate([np.cos(angle), np.sin(angle)], axis=1).astype(jnp.bfloat16)


def twiddle_table():
    angle = 2.0 * np.pi * np.arange(RADIX)[:, None] * np.arange(M)[None, :] / L
    return np.stack([np.cos(angle), np.sin(angle)]).astype(np.float32)


def half_turn_polynomials():
    nodes = 0.5 * np.cos(np.pi * (np.arange(400) + 0.5) / 800)
    square = nodes * nodes
    sine = np.polynomial.polynomial.polyfit(square, np.sin(np.pi * nodes) / nodes, 5)
    cosine = np.polynomial.polynomial.polyfit(square, np.cos(np.pi * nodes), 5)
    return [float(v) for v in sine], [float(v) for v in cosine]


SINE, COSINE = half_turn_polynomials()


def turn_cos_sin(turns):
    r = turns - jnp.floor(turns + 0.5)
    u = r * r
    s = jnp.full_like(u, SINE[-1])
    c = jnp.full_like(u, COSINE[-1])
    for a, b in zip(SINE[-2::-1], COSINE[-2::-1]):
        s = s * u + a
        c = c * u + b
    s = s * r
    twice = s + s
    return 1.0 - twice * s, twice * c


def times_root(re, im, power):
    power = power % 16
    if power == 0:
        return re, im
    if power == 4:
        return -im, re
    if power == 8:
        return -re, -im
    if power == 12:
        return im, -re
    c = math.cos(2.0 * math.pi * power / 16)
    s = math.sin(2.0 * math.pi * power / 16)
    if power in (2, 6, 10, 14):
        a = abs(c)
        plus, minus = (re + im) * a, (re - im) * a
        return {2: (minus, plus), 6: (-plus, minus), 10: (-minus, -plus), 14: (plus, -minus)}[power]
    return re * c - im * s, re * s + im * c


def dft4(v):
    (ar, ai), (br, bi), (cr, ci), (dr, di) = v
    pr, pi_, qr, qi = ar + cr, ai + ci, ar - cr, ai - ci
    sr, si, tr, ti = br + dr, bi + di, br - dr, bi - di
    return [(pr + sr, pi_ + si), (qr - ti, qi + tr), (pr - sr, pi_ - si), (qr + ti, qi - tr)]


def dft16(x):
    inner = []
    for low in range(4):
        inner.append(dft4([x[4 * high + low] for high in range(4)]))
    out = [None] * 16
    for c0 in range(4):
        column = [times_root(*inner[low][c0], low * c0) for low in range(4)]
        for c1, value in enumerate(dft4(column)):
            out[4 * c1 + c0] = value
    return out


def steps_of(step):
    dx, dy, dz = step
    return min(dx, 4 - dx) + min(dy, 4 - dy) + dz


ORDER = sorted(((dx, dy, dz) for dx in range(4) for dy in range(4) for dz in range(2)), key=steps_of, reverse=True)


def kernel(
    off_hbm, own_hbm, tile_hbm, strips_hbm, window_hbm, coords_hbm, table_hbm, twiddle_hbm,
    sub_ref, vis_ref,
    off_ref, own_ref, tile_ref, strips, window_ref, coords_ref, table_ref, twiddle_ref, zb, xt, con, theirs, merged, near, far, grid, row_phase, col_cos, col_sin,
    load_sem, core_s, core_r, near_s, near_r, far_s, far_r, all_s, all_r, fwd_s, fwd_r, oth_s, oth_r,
):
    z = lax.axis_index("frow")
    f = lax.axis_index("fcol")
    core = lax.rem(f, 2)
    chip = f // 2
    x, y = chip // 4, lax.rem(chip, 4)
    side = lax.rem(z, 2)
    ring = z // 2
    sibling = f + 1 - 2 * core

    def loads(part):
        rows = pl.ds(16 * part, 16)
        return pltpu.make_async_copy(strips_hbm.at[:, rows], strips.at[:, rows], load_sem.at[part])

    def whole(src, dst, n):
        return pltpu.make_async_copy(src, dst, load_sem.at[4 + n])

    twiddles = whole(twiddle_hbm, twiddle_ref, 0)
    table = whole(table_hbm, table_ref, 1)
    windows = whole(window_hbm, window_ref, 2)
    coords = whole(coords_hbm, coords_ref, 3)
    offsets = whole(off_hbm, off_ref, 4)
    owners = whole(own_hbm, own_ref, 5)
    tiles = whole(tile_hbm, tile_ref, 6)

    xs = [x] + [lax.rem(x + d, 4) for d in range(1, 4)]
    ys = [y] + [lax.rem(y + d, 4) for d in range(1, 4)]
    chips = [[4 * xs[a] + ys[b] for b in range(4)] for a in range(4)]
    sides = [side, 1 - side]
    rows_of = [[pl.ds(pl.multiple_of(16 * chips[a][b], 16), 16) for b in range(4)] for a in range(4)]
    frows = [z, 2 * ring + 1 - side]
    fcols = [[[2 * chips[a][b] + core, 2 * chips[a][b] + 1 - core] for b in range(4)] for a in range(4)]

    def partner(k, other):
        dx, dy, dz = ORDER[k]
        return {"frow": frows[dz], "fcol": fcols[dx][dy][other]}

    def along(k):
        step = (4, 3, 5, 2, 6, 1, 7)[k]
        return {"frow": 2 * lax.rem(ring + step, FAR) + side, "fcol": f}

    sib = {"frow": z, "fcol": sibling}
    barrier = pltpu.get_barrier_semaphore()

    for k in range(FAR - 1):
        pl.semaphore_signal(barrier, inc=1, device_id=along(k), device_id_type=MESH)

    for k in range(GROUP - 1):
        pl.semaphore_signal(barrier, inc=1, device_id=partner(k, 0), device_id_type=MESH)

    pl.semaphore_signal(barrier, inc=1, device_id=sib, device_id_type=MESH)
    loads(0).start()
    twiddles.start()
    for part in range(1, 4):
        loads(part).start()
    table.start()
    for load in (offsets, windows, coords, owners, tiles):
        load.start()

    def remote(src, dst, send, recv, where):
        return pltpu.make_async_remote_copy(
            src_ref=src, dst_ref=dst, send_sem=send, recv_sem=recv, device_id=where, device_id_type=MESH
        )

    twiddles.wait()
    for part in range(4):
        loads(part).wait()
        rows = pl.ds(16 * part, 16)
        low_rows = pl.ds(ROWS + 16 * part, 16)

        @pl.loop(0, 2)
        def _(half):
            lane = pl.multiple_of(half * 128, 128)
            samples = []
            for g in range(RADIX):
                lanes = pl.ds(pl.multiple_of(M * g + lane, 128), 128)
                samples.append((strips[0, rows, lanes].astype(jnp.float32), strips[1, rows, lanes].astype(jnp.float32)))
            first = pl.ds(lane, 128)
            second = pl.ds(pl.multiple_of(M + lane, 128), 128)
            for c, (re, im) in enumerate(dft16(samples)):
                if c:
                    cos = twiddle_ref[0, pl.ds(c, 1), first]
                    sin = twiddle_ref[1, pl.ds(c, 1), first]
                    re, im = re * cos - im * sin, re * sin + im * cos
                re16, im16 = re.astype(jnp.bfloat16), im.astype(jnp.bfloat16)
                zb[c, rows, first] = re16
                zb[c, rows, second] = -im16
                zb[c, low_rows, first] = im16
                zb[c, low_rows, second] = re16

    table.wait()
    for pair in range(RADIX // 2):
        both = zb[2 * pair : 2 * pair + 2].reshape(2 * 128, 2 * M)
        product = lax.dot_general(
            table_ref[...], both, (((1,), (1,)), ((), ())), preferred_element_type=jnp.float32
        )
        for e in range(2):
            c = 2 * pair + e
            piece = product[:, 128 * e : 128 * e + 128]
            xt[pl.ds(c, M, stride=RADIX), :] = piece
            xt[pl.ds(L + c, M // RADIX, stride=RADIX), :] = piece[: M // RADIX]

    windows.wait()
    offsets.wait()
    window = jnp.transpose(jnp.broadcast_to(window_ref[...], (128, M)))

    for j in range(CHUNKS):
        for q in range(4):
            s = 4 * j + q
            con[s] = (xt[pl.ds(off_ref[s], M), :] * window).astype(jnp.bfloat16)
        if j == 0:
            pl.semaphore_wait(barrier, 1 + (GROUP - 1) + (FAR - 1))
        for e in range(2):
            h = 2 * j + e
            remote(con.at[2 * h + 1 - core], theirs.at[h], core_s.at[h], core_r.at[h], sib).start()

    def near_copy(j, k):
        dx, dy, dz = ORDER[k]
        src = merged.at[2 * j + sides[dz], rows_of[dx][dy]]
        return remote(src, near.at[j, k], near_s.at[j], near_r.at[j], partner(k, 0))

    for j in range(CHUNKS):
        for e in range(2):
            h = 2 * j + e
            remote(con.at[2 * h + 1 - core], theirs.at[h], core_s.at[h], core_r.at[h], sib).wait_recv()
            merged[h] = (con[2 * h + core].astype(jnp.float32) + theirs[h].astype(jnp.float32)).astype(jnp.bfloat16)

        for k in range(GROUP - 1):
            near_copy(j, k).start()

    coords.wait()
    steps = lax.broadcasted_iota(jnp.int32, (TS, 128), 0).astype(jnp.float32)

    @pl.loop(0, VB // 128)
    def _(block):
        lanes = pl.ds(pl.multiple_of(128 * block, 128), 128)
        later = pl.ds(pl.multiple_of(VB + 128 * block, 128), 128)
        for k in range(NB):
            cos, sin = turn_cos_sin(steps * coords_ref[0, k : k + 1, lanes])
            cos, sin = cos.astype(jnp.bfloat16), sin.astype(jnp.bfloat16)
            row_phase[k, 0:TS, lanes] = cos
            row_phase[k, TS : 2 * TS, lanes] = sin
            row_phase[k, 0:TS, later] = -sin
            row_phase[k, TS : 2 * TS, later] = cos
            cos, sin = turn_cos_sin(steps * coords_ref[1, k : k + 1, lanes])
            col_cos[k, :, lanes] = cos
            col_sin[k, :, lanes] = sin

    mine = pl.ds(pl.multiple_of(16 * chip, 16), 16)

    def far_copy(j, k):
        return remote(far.at[j, ring], far.at[j, ring], far_s.at[j], far_r.at[j], along(k))

    def final(j):
        return grid.at[4 * (2 * (2 * j + side) + core) + chip // 4, pl.ds(pl.multiple_of(16 * lax.rem(chip, 4), 16), 16)]

    def all_copy(j, k):
        return remote(final(j), final(j), all_s.at[j], all_r.at[j], partner(k, 0))

    def other_copy(j, where):
        return remote(final(j), final(j), oth_s.at[j], oth_r.at[j], where)

    def fwd_copy(j, e, half):
        at = grid.at[pl.ds(4 * (2 * (2 * j + e) + half), 4)]
        return remote(at, at, fwd_s.at[j, e], fwd_r.at[j, e], sib)

    def wait_for(buffer, sem):
        pltpu.make_async_copy(buffer, buffer, sem).wait()

    for j in range(CHUNKS):
        wait_for(near.at[j, pl.ds(0, GROUP - 1)], near_r.at[j])
        total = merged[2 * j + side, mine].astype(jnp.float32)
        for k in range(GROUP - 1):
            total = total + near[j, k].astype(jnp.float32)
        far[j, ring] = total.astype(jnp.bfloat16)

        for k in range(FAR - 1):
            far_copy(j, k).start()

    scale = 1.0 / math.sqrt(512)
    for j in range(CHUNKS):
        wait_for(far.at[j, pl.ds(0, FAR - 1)], far_r.at[j])
        total = far[j, 0].astype(jnp.float32)
        for k in range(1, FAR):
            total = total + far[j, k].astype(jnp.float32)
        grid[4 * (2 * (2 * j + side) + core) + chip // 4, pl.ds(pl.multiple_of(16 * lax.rem(chip, 4), 16), 16)] = (
            total * scale
        ).astype(jnp.bfloat16)

        for k in range(GROUP - 1):
            all_copy(j, k).start()
            if j in DIRECT:
                other_copy(j, partner(k, 1)).start()

        if j in DIRECT:
            other_copy(j, sib).start()

    for j in range(CHUNKS):
        wait_for(near.at[j, pl.ds(0, GROUP - 1)], all_r.at[j])
        if j not in DIRECT:
            for e in range(2):
                fwd_copy(j, e, core).start()

    for j in range(CHUNKS):
        if j in DIRECT:
            wait_for(grid.at[pl.ds(0, 8)], oth_r.at[j])
        else:
            for e in range(2):
                fwd_copy(j, e, 1 - core).wait_recv()

    owners.wait()
    tiles.wait()
    count = jnp.int32(0)
    place = [jnp.int32(0)] * CAP
    for s in range(S):
        hit = (own_ref[s] == z).astype(jnp.int32)
        for slot in range(CAP):
            place[slot] = place[slot] + jnp.where((hit == 1) & (count == slot), s, 0)
        count = count + hit
    for slot in range(CAP):
        picked = grid[pl.ds(4 * place[slot], 4)].reshape(M, 2 * ROWS).astype(jnp.float32)
        picked = jnp.where(count > slot, picked, 0.0)
        sub_ref[slot] = jnp.transpose(picked).astype(jnp.bfloat16)

    for k in range(NB):
        tile = grid[tile_ref[k]]
        half = jnp.dot(tile, row_phase[k], preferred_element_type=jnp.float32)
        re, im = half[:, :VB], half[:, VB:]
        cos, sin = col_cos[k], col_sin[k]
        vis_ref[0, pl.ds(k, 1)] = jnp.sum(re * cos + im * sin, axis=0, keepdims=True) * (1.0 / TS)
        vis_ref[1, pl.ds(k, 1)] = jnp.sum(im * cos - re * sin, axis=0, keepdims=True) * (1.0 / TS)

    for j in range(CHUNKS):
        for e in range(2):
            h = 2 * j + e
            remote(con.at[2 * h + 1 - core], theirs.at[h], core_s.at[h], core_r.at[h], sib).wait_send()
            if j not in DIRECT:
                fwd_copy(j, e, core).wait_send()
        if j in DIRECT:
            wait_for(grid.at[pl.ds(0, 8)], oth_s.at[j])
        wait_for(near.at[j, pl.ds(0, GROUP - 1)], near_s.at[j])
        wait_for(far.at[j, pl.ds(0, FAR - 1)], far_s.at[j])
        wait_for(near.at[j, pl.ds(0, GROUP - 1)], all_s.at[j])


def write_out(sub_ref, vis_ref, sub_hbm, vis_hbm, sems):
    copies = [
        pltpu.make_async_copy(sub_ref, sub_hbm, sems.at[0]),
        pltpu.make_async_copy(vis_ref, vis_hbm, sems.at[1]),
    ]
    for copy in copies:
        copy.start()
    for copy in copies:
        copy.wait()


def on_device(strips, facet_window, sub_offset, sub_owner, block_tile, vis_coords):
    vmem = pl.BlockSpec(memory_space=pltpu.VMEM)
    dma = pltpu.SemaphoreType.DMA
    bf16, f32 = jnp.bfloat16, jnp.float32
    subgrids, visibilities = pl.pallas_call(
        kernel,
        out_shape=(
            pltpu.VMEM((CAP, 2 * ROWS, M), bf16),
            pltpu.VMEM((2, NB, VB), f32),
        ),
        in_specs=[pl.BlockSpec(memory_space=pltpu.HBM)] * 8,
        out_specs=(vmem, vmem),
        scratch_shapes=[
            pltpu.SMEM((S,), jnp.int32),
            pltpu.SMEM((S,), jnp.int32),
            pltpu.SMEM((NB,), jnp.int32),
            pltpu.VMEM((2, ROWS, L), bf16),
            pltpu.VMEM((1, M), f32),
            pltpu.VMEM((2, NB, VB), f32),
            pltpu.VMEM((M, 2 * M), bf16),
            pltpu.VMEM((2, RADIX, M), f32),
            pltpu.VMEM((RADIX, 2 * ROWS, 2 * M), bf16),
            pltpu.VMEM((L + M, 2 * ROWS), f32),
            pltpu.VMEM((S, M, 2 * ROWS), bf16),
            pltpu.VMEM((S // 2, M, 2 * ROWS), bf16),
            pltpu.VMEM((S // 2, M, 2 * ROWS), bf16),
            pltpu.VMEM((CHUNKS, GROUP - 1, 16, 2 * ROWS), bf16),
            pltpu.VMEM((CHUNKS, FAR, 16, 2 * ROWS), bf16),
            pltpu.VMEM((4 * S, TS, 2 * ROWS), bf16),
            pltpu.VMEM((NB, 2 * TS, 2 * VB), bf16),
            pltpu.VMEM((NB, TS, VB), f32),
            pltpu.VMEM((NB, TS, VB), f32),
            dma((11,)),
            dma((S // 2,)), dma((S // 2,)),
            dma((CHUNKS,)), dma((CHUNKS,)),
            dma((CHUNKS,)), dma((CHUNKS,)),
            dma((CHUNKS,)), dma((CHUNKS,)),
            dma((CHUNKS, 2)), dma((CHUNKS, 2)),
            dma((CHUNKS,)), dma((CHUNKS,)),
        ],
        compiler_params=pltpu.CompilerParams(
            collective_id=0, has_side_effects=True, vmem_limit_bytes=60 * 2**20
        ),
        name="predict",
    )(
        sub_offset, sub_owner, block_tile, strips.reshape(2, ROWS, L), facet_window.reshape(1, M), vis_coords,
        jnp.asarray(dft_table()), jnp.asarray(twiddle_table()),
    )
    subgrids, visibilities = pl.pallas_call(
        write_out,
        out_shape=(
            jax.ShapeDtypeStruct((CAP, 2 * ROWS, M), bf16),
            jax.ShapeDtypeStruct((2, NB, VB), f32),
        ),
        in_specs=[vmem, vmem],
        out_specs=(pl.BlockSpec(memory_space=pltpu.HBM), pl.BlockSpec(memory_space=pltpu.HBM)),
        scratch_shapes=[dma((2,))],
        compiler_params=pltpu.CompilerParams(vmem_limit_bytes=2**20),
        name="write_out",
    )(subgrids, visibilities)
    return subgrids.reshape(1, CAP, 2, ROWS, M), visibilities


def solution(mesh):
    placed = (
        P(None, "frow", "fcol", None, None),
        P("frow", "fcol", None),
        P(),
        P(),
        P(("frow", "fcol")),
        P(None, ("frow", "fcol"), None),
    )
    return jax.shard_map(
        on_device,
        mesh=mesh,
        in_specs=placed,
        out_specs=(P("frow", None, None, None, None), P(None, ("frow", "fcol"), None)),
        check_vma=False,
    )
```

```python
import math

import jax
import jax.numpy as jnp
import numpy as np
from jax import lax
from jax.experimental import pallas as pl
from jax.experimental.pallas import tpu as pltpu
from jax.sharding import PartitionSpec as P

MESH = pl.DeviceIdType.MESH
TS = 64
CAP = 2
ROWS = 64
M = 256
L = 4096
S = 12
RADIX = 16
NB = 4
VB = 512
CHUNKS = 3
GROUP = 32
FAR = 8
DIRECT = (2,)


def dft_table():
    index = np.arange(M)
    angle = 2.0 * np.pi * ((index[:, None] * index[None, :]) % M) / M
    return np.concatenate([np.cos(angle), np.sin(angle)], axis=1).astype(jnp.bfloat16)


def twiddle_table():
    angle = 2.0 * np.pi * np.arange(RADIX)[:, None] * np.arange(M)[None, :] / L
    return np.stack([np.cos(angle), np.sin(angle)]).astype(np.float32)


def half_turn_polynomials():
    nodes = 0.5 * np.cos(np.pi * (np.arange(400) + 0.5) / 800)
    square = nodes * nodes
    sine = np.polynomial.polynomial.polyfit(square, np.sin(np.pi * nodes) / nodes, 5)
    cosine = np.polynomial.polynomial.polyfit(square, np.cos(np.pi * nodes), 5)
    return [float(v) for v in sine], [float(v) for v in cosine]


SINE, COSINE = half_turn_polynomials()


def turn_cos_sin(turns):
    r = turns - jnp.floor(turns + 0.5)
    u = r * r
    s = jnp.full_like(u, SINE[-1])
    c = jnp.full_like(u, COSINE[-1])
    for a, b in zip(SINE[-2::-1], COSINE[-2::-1]):
        s = s * u + a
        c = c * u + b
    s = s * r
    twice = s + s
    return 1.0 - twice * s, twice * c


def times_root(re, im, power):
    power = power % 16
    if power == 0:
        return re, im
    if power == 4:
        return -im, re
    if power == 8:
        return -re, -im
    if power == 12:
        return im, -re
    c = math.cos(2.0 * math.pi * power / 16)
    s = math.sin(2.0 * math.pi * power / 16)
    if power in (2, 6, 10, 14):
        a = abs(c)
        plus, minus = (re + im) * a, (re - im) * a
        return {2: (minus, plus), 6: (-plus, minus), 10: (-minus, -plus), 14: (plus, -minus)}[power]
    return re * c - im * s, re * s + im * c


def dft4(v):
    (ar, ai), (br, bi), (cr, ci), (dr, di) = v
    pr, pi_, qr, qi = ar + cr, ai + ci, ar - cr, ai - ci
    sr, si, tr, ti = br + dr, bi + di, br - dr, bi - di
    return [(pr + sr, pi_ + si), (qr - ti, qi + tr), (pr - sr, pi_ - si), (qr + ti, qi - tr)]


def dft16(x):
    inner = []
    for low in range(4):
        inner.append(dft4([x[4 * high + low] for high in range(4)]))
    out = [None] * 16
    for c0 in range(4):
        column = [times_root(*inner[low][c0], low * c0) for low in range(4)]
        for c1, value in enumerate(dft4(column)):
            out[4 * c1 + c0] = value
    return out


def steps_of(step):
    dx, dy, dz = step
    return min(dx, 4 - dx) + min(dy, 4 - dy) + dz


ORDER = sorted(((dx, dy, dz) for dx in range(4) for dy in range(4) for dz in range(2)), key=steps_of, reverse=True)


def kernel(
    off_hbm, own_hbm, tile_hbm, strips_hbm, window_hbm, coords_hbm, table_hbm, twiddle_hbm,
    sub_ref, vis_ref,
    off_ref, own_ref, tile_ref, strips, window_ref, coords_ref, table_ref, twiddle_ref, zb, xt, con, theirs, merged, near, far, grid, row_phase, col_cos, col_sin,
    load_sem, core_s, core_r, near_s, near_r, far_s, far_r, all_s, all_r, fwd_s, fwd_r, oth_s, oth_r,
):
    z = lax.axis_index("frow")
    f = lax.axis_index("fcol")
    core = lax.rem(f, 2)
    chip = f // 2
    x, y = chip // 4, lax.rem(chip, 4)
    side = lax.rem(z, 2)
    ring = z // 2
    sibling = f + 1 - 2 * core

    def loads(part):
        rows = pl.ds(16 * part, 16)
        return pltpu.make_async_copy(strips_hbm.at[:, rows], strips.at[:, rows], load_sem.at[part])

    def whole(src, dst, n):
        return pltpu.make_async_copy(src, dst, load_sem.at[4 + n])

    twiddles = whole(twiddle_hbm, twiddle_ref, 0)
    table = whole(table_hbm, table_ref, 1)
    windows = whole(window_hbm, window_ref, 2)
    coords = whole(coords_hbm, coords_ref, 3)
    offsets = whole(off_hbm, off_ref, 4)
    owners = whole(own_hbm, own_ref, 5)
    tiles = whole(tile_hbm, tile_ref, 6)
    loads(0).start()
    twiddles.start()
    for part in range(1, 4):
        loads(part).start()
    table.start()

    xs = [x] + [lax.rem(x + d, 4) for d in range(1, 4)]
    ys = [y] + [lax.rem(y + d, 4) for d in range(1, 4)]
    chips = [[4 * xs[a] + ys[b] for b in range(4)] for a in range(4)]
    sides = [side, 1 - side]
    rows_of = [[pl.ds(pl.multiple_of(16 * chips[a][b], 16), 16) for b in range(4)] for a in range(4)]
    frows = [z, 2 * ring + 1 - side]
    fcols = [[[2 * chips[a][b] + core, 2 * chips[a][b] + 1 - core] for b in range(4)] for a in range(4)]

    def partner(k, other):
        dx, dy, dz = ORDER[k]
        return {"frow": frows[dz], "fcol": fcols[dx][dy][other]}

    def along(k):
        step = (4, 3, 5, 2, 6, 1, 7)[k]
        return {"frow": 2 * lax.rem(ring + step, FAR) + side, "fcol": f}

    sib = {"frow": z, "fcol": sibling}
    barrier = pltpu.get_barrier_semaphore()

    for k in range(FAR - 1):
        pl.semaphore_signal(barrier, inc=1, device_id=along(k), device_id_type=MESH)

    for k in range(GROUP - 1):
        pl.semaphore_signal(barrier, inc=1, device_id=partner(k, 0), device_id_type=MESH)
        pl.semaphore_signal(barrier, inc=1, device_id=partner(k, 1), device_id_type=MESH)

    pl.semaphore_signal(barrier, inc=1, device_id=sib, device_id_type=MESH)
    for load in (offsets, windows, coords, owners, tiles):
        load.start()

    def remote(src, dst, send, recv, where):
        return pltpu.make_async_remote_copy(
            src_ref=src, dst_ref=dst, send_sem=send, recv_sem=recv, device_id=where, device_id_type=MESH
        )

    twiddles.wait()
    for part in range(4):
        loads(part).wait()
        rows = pl.ds(16 * part, 16)
        low_rows = pl.ds(ROWS + 16 * part, 16)

        @pl.loop(0, 2)
        def _(half):
            lane = pl.multiple_of(half * 128, 128)
            samples = []
            for g in range(RADIX):
                lanes = pl.ds(pl.multiple_of(M * g + lane, 128), 128)
                samples.append((strips[0, rows, lanes].astype(jnp.float32), strips[1, rows, lanes].astype(jnp.float32)))
            first = pl.ds(lane, 128)
            second = pl.ds(pl.multiple_of(M + lane, 128), 128)
            for c, (re, im) in enumerate(dft16(samples)):
                if c:
                    cos = twiddle_ref[0, pl.ds(c, 1), first]
                    sin = twiddle_ref[1, pl.ds(c, 1), first]
                    re, im = re * cos - im * sin, re * sin + im * cos
                re16, im16 = re.astype(jnp.bfloat16), im.astype(jnp.bfloat16)
                zb[c, rows, first] = re16
                zb[c, rows, second] = -im16
                zb[c, low_rows, first] = im16
                zb[c, low_rows, second] = re16

    table.wait()
    for pair in range(RADIX // 2):
        both = zb[2 * pair : 2 * pair + 2].reshape(2 * 128, 2 * M)
        product = lax.dot_general(
            table_ref[...], both, (((1,), (1,)), ((), ())), preferred_element_type=jnp.float32
        )
        for e in range(2):
            c = 2 * pair + e
            piece = product[:, 128 * e : 128 * e + 128]
            xt[pl.ds(c, M, stride=RADIX), :] = piece
            xt[pl.ds(L + c, M // RADIX, stride=RADIX), :] = piece[: M // RADIX]

    windows.wait()
    offsets.wait()
    window = jnp.transpose(jnp.broadcast_to(window_ref[...], (128, M)))

    for j in range(CHUNKS):
        for q in range(4):
            s = 4 * j + q
            con[s] = (xt[pl.ds(off_ref[s], M), :] * window).astype(jnp.bfloat16)
        if j == 0:
            pl.semaphore_wait(barrier, 1 + 2 * (GROUP - 1) + (FAR - 1))
        for e in range(2):
            h = 2 * j + e
            remote(con.at[2 * h + 1 - core], theirs.at[h], core_s.at[h], core_r.at[h], sib).start()

    def near_copy(j, k):
        dx, dy, dz = ORDER[k]
        src = merged.at[2 * j + sides[dz], rows_of[dx][dy]]
        return remote(src, near.at[j, k], near_s.at[j], near_r.at[j], partner(k, 0))

    for j in range(CHUNKS):
        for e in range(2):
            h = 2 * j + e
            remote(con.at[2 * h + 1 - core], theirs.at[h], core_s.at[h], core_r.at[h], sib).wait_recv()
            merged[h] = (con[2 * h + core].astype(jnp.float32) + theirs[h].astype(jnp.float32)).astype(jnp.bfloat16)

        for k in range(GROUP - 1):
            near_copy(j, k).start()

    coords.wait()
    steps = lax.broadcasted_iota(jnp.int32, (TS, 128), 0).astype(jnp.float32)

    @pl.loop(0, VB // 128)
    def _(block):
        lanes = pl.ds(pl.multiple_of(128 * block, 128), 128)
        later = pl.ds(pl.multiple_of(VB + 128 * block, 128), 128)
        for k in range(NB):
            cos, sin = turn_cos_sin(steps * coords_ref[0, k : k + 1, lanes])
            cos, sin = cos.astype(jnp.bfloat16), sin.astype(jnp.bfloat16)
            row_phase[k, 0:TS, lanes] = cos
            row_phase[k, TS : 2 * TS, lanes] = sin
            row_phase[k, 0:TS, later] = -sin
            row_phase[k, TS : 2 * TS, later] = cos
            cos, sin = turn_cos_sin(steps * coords_ref[1, k : k + 1, lanes])
            col_cos[k, :, lanes] = cos
            col_sin[k, :, lanes] = sin

    mine = pl.ds(pl.multiple_of(16 * chip, 16), 16)

    def far_copy(j, k):
        return remote(far.at[j, ring], far.at[j, ring], far_s.at[j], far_r.at[j], along(k))

    def final(j):
        return grid.at[4 * (2 * (2 * j + side) + core) + chip // 4, pl.ds(pl.multiple_of(16 * lax.rem(chip, 4), 16), 16)]

    def all_copy(j, k):
        return remote(final(j), final(j), all_s.at[j], all_r.at[j], partner(k, 0))

    def other_copy(j, where):
        return remote(final(j), final(j), oth_s.at[j], oth_r.at[j], where)

    def fwd_copy(j, e, half):
        at = grid.at[pl.ds(4 * (2 * (2 * j + e) + half), 4)]
        return remote(at, at, fwd_s.at[j, e], fwd_r.at[j, e], sib)

    def wait_for(buffer, sem):
        pltpu.make_async_copy(buffer, buffer, sem).wait()

    for j in range(CHUNKS):
        wait_for(near.at[j, pl.ds(0, GROUP - 1)], near_r.at[j])
        total = merged[2 * j + side, mine].astype(jnp.float32)
        for k in range(GROUP - 1):
            total = total + near[j, k].astype(jnp.float32)
        far[j, ring] = total.astype(jnp.bfloat16)

        for k in range(FAR - 1):
            far_copy(j, k).start()

    scale = 1.0 / math.sqrt(512)
    for j in range(CHUNKS):
        wait_for(far.at[j, pl.ds(0, FAR - 1)], far_r.at[j])
        total = far[j, 0].astype(jnp.float32)
        for k in range(1, FAR):
            total = total + far[j, k].astype(jnp.float32)
        grid[4 * (2 * (2 * j + side) + core) + chip // 4, pl.ds(pl.multiple_of(16 * lax.rem(chip, 4), 16), 16)] = (
            total * scale
        ).astype(jnp.bfloat16)

        for k in range(GROUP - 1):
            all_copy(j, k).start()

        if j in DIRECT:
            for k in range(GROUP - 1):
                other_copy(j, partner(k, 1)).start()
            other_copy(j, sib).start()

    for j in range(CHUNKS):
        wait_for(near.at[j, pl.ds(0, GROUP - 1)], all_r.at[j])
        if j not in DIRECT:
            for e in range(2):
                fwd_copy(j, e, core).start()

    for j in range(CHUNKS):
        if j in DIRECT:
            wait_for(grid.at[pl.ds(0, 8)], oth_r.at[j])
        else:
            for e in range(2):
                fwd_copy(j, e, 1 - core).wait_recv()

    owners.wait()
    tiles.wait()
    count = jnp.int32(0)
    place = [jnp.int32(0)] * CAP
    for s in range(S):
        hit = (own_ref[s] == z).astype(jnp.int32)
        for slot in range(CAP):
            place[slot] = place[slot] + jnp.where((hit == 1) & (count == slot), s, 0)
        count = count + hit
    for slot in range(CAP):
        picked = grid[pl.ds(4 * place[slot], 4)].reshape(M, 2 * ROWS).astype(jnp.float32)
        picked = jnp.where(count > slot, picked, 0.0)
        sub_ref[slot] = jnp.transpose(picked).astype(jnp.bfloat16)

    for k in range(NB):
        tile = grid[tile_ref[k]]
        half = jnp.dot(tile, row_phase[k], preferred_element_type=jnp.float32)
        re, im = half[:, :VB], half[:, VB:]
        cos, sin = col_cos[k], col_sin[k]
        vis_ref[0, pl.ds(k, 1)] = jnp.sum(re * cos + im * sin, axis=0, keepdims=True) * (1.0 / TS)
        vis_ref[1, pl.ds(k, 1)] = jnp.sum(im * cos - re * sin, axis=0, keepdims=True) * (1.0 / TS)

    for j in range(CHUNKS):
        for e in range(2):
            h = 2 * j + e
            remote(con.at[2 * h + 1 - core], theirs.at[h], core_s.at[h], core_r.at[h], sib).wait_send()
            if j not in DIRECT:
                fwd_copy(j, e, core).wait_send()
        if j in DIRECT:
            wait_for(grid.at[pl.ds(0, 8)], oth_s.at[j])
        wait_for(near.at[j, pl.ds(0, GROUP - 1)], near_s.at[j])
        wait_for(far.at[j, pl.ds(0, FAR - 1)], far_s.at[j])
        wait_for(near.at[j, pl.ds(0, GROUP - 1)], all_s.at[j])


def write_out(sub_ref, vis_ref, sub_hbm, vis_hbm, sems):
    copies = [
        pltpu.make_async_copy(sub_ref, sub_hbm, sems.at[0]),
        pltpu.make_async_copy(vis_ref, vis_hbm, sems.at[1]),
    ]
    for copy in copies:
        copy.start()
    for copy in copies:
        copy.wait()


def on_device(strips, facet_window, sub_offset, sub_owner, block_tile, vis_coords):
    vmem = pl.BlockSpec(memory_space=pltpu.VMEM)
    dma = pltpu.SemaphoreType.DMA
    bf16, f32 = jnp.bfloat16, jnp.float32
    subgrids, visibilities = pl.pallas_call(
        kernel,
        out_shape=(
            pltpu.VMEM((CAP, 2 * ROWS, M), bf16),
            pltpu.VMEM((2, NB, VB), f32),
        ),
        in_specs=[pl.BlockSpec(memory_space=pltpu.HBM)] * 8,
        out_specs=(vmem, vmem),
        scratch_shapes=[
            pltpu.SMEM((S,), jnp.int32),
            pltpu.SMEM((S,), jnp.int32),
            pltpu.SMEM((NB,), jnp.int32),
            pltpu.VMEM((2, ROWS, L), bf16),
            pltpu.VMEM((1, M), f32),
            pltpu.VMEM((2, NB, VB), f32),
            pltpu.VMEM((M, 2 * M), bf16),
            pltpu.VMEM((2, RADIX, M), f32),
            pltpu.VMEM((RADIX, 2 * ROWS, 2 * M), bf16),
            pltpu.VMEM((L + M, 2 * ROWS), f32),
            pltpu.VMEM((S, M, 2 * ROWS), bf16),
            pltpu.VMEM((S // 2, M, 2 * ROWS), bf16),
            pltpu.VMEM((S // 2, M, 2 * ROWS), bf16),
            pltpu.VMEM((CHUNKS, GROUP - 1, 16, 2 * ROWS), bf16),
            pltpu.VMEM((CHUNKS, FAR, 16, 2 * ROWS), bf16),
            pltpu.VMEM((4 * S, TS, 2 * ROWS), bf16),
            pltpu.VMEM((NB, 2 * TS, 2 * VB), bf16),
            pltpu.VMEM((NB, TS, VB), f32),
            pltpu.VMEM((NB, TS, VB), f32),
            dma((11,)),
            dma((S // 2,)), dma((S // 2,)),
            dma((CHUNKS,)), dma((CHUNKS,)),
            dma((CHUNKS,)), dma((CHUNKS,)),
            dma((CHUNKS,)), dma((CHUNKS,)),
            dma((CHUNKS, 2)), dma((CHUNKS, 2)),
            dma((CHUNKS,)), dma((CHUNKS,)),
        ],
        compiler_params=pltpu.CompilerParams(
            collective_id=0, has_side_effects=True, vmem_limit_bytes=60 * 2**20
        ),
        name="predict",
    )(
        sub_offset, sub_owner, block_tile, strips.reshape(2, ROWS, L), facet_window.reshape(1, M), vis_coords,
        jnp.asarray(dft_table()), jnp.asarray(twiddle_table()),
    )
    subgrids, visibilities = pl.pallas_call(
        write_out,
        out_shape=(
            jax.ShapeDtypeStruct((CAP, 2 * ROWS, M), bf16),
            jax.ShapeDtypeStruct((2, NB, VB), f32),
        ),
        in_specs=[vmem, vmem],
        out_specs=(pl.BlockSpec(memory_space=pltpu.HBM), pl.BlockSpec(memory_space=pltpu.HBM)),
        scratch_shapes=[dma((2,))],
        compiler_params=pltpu.CompilerParams(vmem_limit_bytes=2**20),
        name="write_out",
    )(subgrids, visibilities)
    return subgrids.reshape(1, CAP, 2, ROWS, M), visibilities


def solution(mesh):
    placed = (
        P(None, "frow", "fcol", None, None),
        P("frow", "fcol", None),
        P(),
        P(),
        P(("frow", "fcol")),
        P(None, ("frow", "fcol"), None),
    )
    return jax.shard_map(
        on_device,
        mesh=mesh,
        in_specs=placed,
        out_specs=(P("frow", None, None, None, None), P(None, ("frow", "fcol"), None)),
        check_vma=False,
    )
```
